128 devices in a mesh: dp: 8 (over x, z_lo), vocab: 16 (over z_hi, y, core).
Axes of the slice: x: 4, y: 4, z: 4 (z_hi: 2, z_lo: 2; z = z_hi * 2 + z_lo), core: 2. Of those that a mesh axis runs over, the one named last changes fastest.
Arguments:
- hidden_rows: bfloat16 [768, 5120], P('dp')
- head_weight: bfloat16 [5120, 81920], P(None, ('dp', 'vocab')), may hold values from -0.625 to 0.625
- teacher_logits: bfloat16 [768, 81920], P(('dp', 'vocab'))
- upstream: float32 [768], replicated, may hold values from 2000 to 20000
- block_map: int32 [32], replicated, may hold values from 0 to 31, each once
- token_order: int32 [768], replicated, may hold values from 0 to 767, each once
Outputs:
- grad_head: bfloat16 [5120, 81920], P(None, ('dp', 'vocab'))
- grad_hidden: bfloat16 [768, 5120], P(('dp', 'vocab'))
The draws below stay inside these ranges and needn't reach their ends.
Inputs may be any that keep to these rules, and one draw needn't show every extreme that they name: block_map is a permutation of the 32 blocks. token_order is a permutation of the 768 tokens.
All inputs are finite; a program needn't handle non-finite values.
Results may differ from the reference program's by a relative error of at most 0.0071.
Values may be sent and summed in bfloat16 or wider, within the bound.
A program may use at most 128 MiB of HBM per device.

```python
import math
import jax
import jax.numpy as jnp
from jax import lax

D = 5120
TSH = 32
TOKENS = 768
V = 81920


def draw_hidden_rows(key, part):
    key = jax.random.fold_in(key, 11)
    first, second = jax.random.split(key)
    scale = jnp.exp(jax.random.uniform(second, (TOKENS, 1), minval=math.log(0.5), maxval=math.log(4.0)))
    values = jax.random.truncated_normal(first, -6.0, 6.0, (TOKENS, D)) * scale * 0.05
    return values.astype(jnp.float32).astype(jnp.bfloat16)


def draw_teacher_logits(key, part):
    key = jax.random.fold_in(key, 23)
    first, second = jax.random.split(key)
    scale = jnp.exp(jax.random.uniform(second, (TOKENS, 1), minval=math.log(0.5), maxval=math.log(2.0)))
    values = jax.random.truncated_normal(first, -6.0, 6.0, (TOKENS, V)) * 0.3 * scale
    return values.astype(jnp.float32).astype(jnp.bfloat16)


def block_scale(rng, extent, pieces, least, high):
    gain, own = 1.0, jax.random.fold_in(rng, 6)
    for dim, shards_of in pieces:
        steps = jnp.exp(jax.random.uniform(jax.random.fold_in(own, dim), (shards_of,), jnp.float32, least / len(pieces), high / len(pieces)))
        gain = gain * jnp.repeat(steps, extent[dim] // shards_of).reshape([-1 if axis == dim else 1 for axis in range(len(extent))])
    return gain


def bell_draw(own_key, extent, width, most, cuts=(), kind=jnp.bfloat16):
    drawn = jax.random.normal(own_key, extent, jnp.float32) * width
    if len(cuts) > 0:
        drawn = block_scale(own_key, extent, cuts, -0.22, 0.18) * drawn
    return jnp.clip(drawn, min=-most, max=most).astype(kind)


def setup_inputs(seed: int = 0) -> dict:
    key_list = jax.random.split(jax.random.key(seed), 7)
    hidden_rows = draw_hidden_rows(jax.random.fold_in(key_list[6], 71), 0)
    head_weight = bell_draw(key_list[1], (D, V), (3.0 / D ** 0.5), 0.625, ((1, 128),))
    teacher_logits = draw_teacher_logits(jax.random.fold_in(key_list[6], 71), 0)
    upstream = jnp.clip(jnp.exp(jax.random.uniform(key_list[3], (TOKENS,), jnp.float32, math.log(2000.0), math.log(20000.0))), 2000.0, 20000.0)
    block_map = jax.random.permutation(key_list[4], TSH).astype(jnp.int32)
    token_order = jax.random.permutation(key_list[5], TOKENS).astype(jnp.int32)
    return {"hidden_rows": hidden_rows, "head_weight": head_weight, "teacher_logits": teacher_logits, "upstream": upstream, "block_map": block_map, "token_order": token_order}


def reference(hidden_rows, head_weight, teacher_logits, upstream, block_map, token_order):
    logits = jnp.dot(hidden_rows, head_weight, preferred_element_type=jnp.float32)
    row_max = jnp.max(logits, axis=1, keepdims=True)
    shifted = jnp.exp(logits - row_max)
    row_total = jnp.sum(shifted, axis=1, keepdims=True)
    teacher_probs = jax.nn.softmax(teacher_logits.astype(jnp.float32), axis=1).astype(jnp.bfloat16)
    blocks = teacher_probs.reshape(TOKENS, TSH, V // TSH)
    aligned = jnp.take(blocks, block_map, axis=1).reshape(TOKENS, V)
    logit_grad = (upstream[:, None] * (shifted / row_total - aligned.astype(jnp.float32))).astype(jnp.bfloat16)
    grad_head = lax.dot_general(hidden_rows, logit_grad, (((0,), (0,)), ((), ())), preferred_element_type=jnp.float32).astype(jnp.bfloat16)
    grad_full = lax.dot_general(logit_grad, head_weight, (((1,), (1,)), ((), ())), preferred_element_type=jnp.float32)
    grad_hidden = jnp.take(grad_full, token_order, axis=0).astype(jnp.bfloat16)
    return grad_head, grad_hidden
```

```python
import jax
import jax.numpy as jnp
from jax import lax
from jax.experimental import pallas as pl
from jax.experimental.pallas import tpu as pltpu
from jax.sharding import PartitionSpec as P

MESH = pl.DeviceIdType.MESH
F32 = jnp.float32
BF16 = jnp.bfloat16
HALF = 2560
XW, YW, ZW = 512, 256, 1024
Y0, Z0 = 512, 1536
LANES = ((0, (512, 384)), (896, (512, 384)), (1792, (384, 384)))


def device(x, y, z, c):
    return (x * 2 + lax.rem(z, 2), (z // 2) * 8 + y * 2 + c)


def teacher_kernel(bmap, t_ref, o_ref):
    width = 2560

    def top(j, m):
        cols = pl.ds(pl.multiple_of(j * width, width), width)
        return jnp.maximum(m, jnp.max(t_ref[:, cols].astype(F32), axis=1, keepdims=True))

    m = lax.fori_loop(0, 32, top, jnp.full((6, 1), -jnp.inf, F32))

    def add(j, s):
        cols = pl.ds(pl.multiple_of(j * width, width), width)
        return s + jnp.sum(jnp.exp(t_ref[:, cols].astype(F32) - m), axis=1, keepdims=True)

    s = lax.fori_loop(0, 32, add, jnp.zeros((6, 1), F32))
    pad = jnp.zeros((2, 128), F32)

    def block(j, carry):
        cols = pl.ds(pl.multiple_of(bmap[j] * width, width), width)
        p = jnp.exp(t_ref[:, cols].astype(F32) - m) / s
        for k in range(4):
            rows = [p[:, 640 * k + 128 * i : 640 * k + 128 * i + 128] for i in range(5)]
            o_ref[4 * j + k] = jnp.concatenate(rows + [pad], axis=0).astype(BF16)
        return carry

    lax.fori_loop(0, 32, block, 0)


def head_kernel(
    hid, w, tea, ups, tok, gh, gx,
    hb, wb, ws, acc, qb, rt, g, st0, st1, st2, perm, gp, gs, ghb, fin, fs,
    t00, t01, t10, t11, t20, t21, a00, a01, a10, a11, a20, a21,
    u00, u01, u10, u11, u20, u21, b00, b01, b10, b11, b20, b21,
    v00, v01, v10, v11, v20, v21, c00, c01, c10, c11, c20, c21,
    ss, rs, ls, tss, trs,
):
    tps = ((t00, t01), (t10, t11), (t20, t21))
    ras = ((a00, a01), (a10, a11), (a20, a21))
    tbs = ((u00, u01), (u10, u11), (u20, u21))
    rbs = ((b00, b01), (b10, b11), (b20, b21))
    tcs = ((v00, v01), (v10, v11), (v20, v21))
    rcs = ((c00, c01), (c10, c11), (c20, c21))
    dp = lax.axis_index("dp")
    vo = lax.axis_index("vocab")
    x, zl = dp // 2, lax.rem(dp, 2)
    zh, y, c = vo // 8, lax.rem(vo // 2, 4), lax.rem(vo, 2)
    z = zh * 2 + zl
    o = 1 - c
    me = dp * 16 + vo

    def rot(v, d):
        return lax.rem(v + d, 4)

    def xn(d):
        return device(rot(x, d), y, z, c)

    def yn(d):
        return device(x, rot(y, d), z, c)

    def zn(d):
        return device(x, y, rot(z, d), c)

    sib = device(x, y, z, o)
    sent = []

    def send(src, dst, to):
        k = len(sent)
        cp = pltpu.make_async_remote_copy(
            src_ref=src, dst_ref=dst, send_sem=ss.at[k], recv_sem=rs.at[k],
            device_id=to, device_id_type=MESH,
        )
        cp.start()
        sent.append(cp)
        return cp

    def arrive(*cps):
        for cp in cps:
            cp.wait_recv()

    q0, qo = 2 * zl, 2 * (1 - zl)
    mine = pl.multiple_of(HALF * c, 128)
    own = (
        pltpu.make_async_copy(hid.at[:, :, pl.ds(mine, XW)], hb.at[c, x, pl.ds(q0, 2), :, pl.ds(0, XW)], ls.at[0]),
        pltpu.make_async_copy(
            hid.at[:, :, pl.ds(pl.multiple_of(mine + Y0 + YW * y, 128), YW)],
            hb.at[c, x, pl.ds(q0, 2), :, pl.ds(pl.multiple_of(Y0 + YW * y, 128), YW)], ls.at[14]),
        pltpu.make_async_copy(
            hid.at[zh, :, pl.ds(pl.multiple_of(mine + Z0, 128), ZW)],
            hb.at[c, x, q0 + zh, :, pl.ds(Z0, ZW)], ls.at[15]),
    )
    for cp in own:
        cp.start()
    other = pltpu.make_async_copy(
        hid.at[:, :, pl.ds(pl.multiple_of(HALF * o, 128), XW)],
        hb.at[o, x, pl.ds(q0, 2), :, pl.ds(0, XW)], ls.at[1])
    other.start()
    wcopy = pltpu.make_async_copy(w, wb, ls.at[2])
    wcopy.start()
    tcopy = pltpu.make_async_copy(tea.at[me], rt.at[me], ls.at[3])
    tcopy.start()

    bar = pltpu.get_barrier_semaphore()

    def greet(i, carry):
        t = lax.rem(me + i, 128)
        pl.semaphore_signal(bar, inc=1, device_id=(t // 16, lax.rem(t, 16)), device_id_type=MESH)
        return carry

    lax.fori_loop(1, 128, greet, 0)
    pl.semaphore_wait(bar, 127)
    for cp in own:
        cp.wait()

    def ysl(yy):
        return pl.ds(pl.multiple_of(Y0 + YW * yy, 128), YW)

    def zq(zz):
        return 2 * lax.rem(zz, 2) + zz // 2

    def same(ref, to):
        return send(ref, ref, to)

    xs, zs = pl.ds(0, XW), pl.ds(Z0, ZW)
    px = (same(hb.at[c, x, q0, :, xs], zn(1)), same(hb.at[c, x, q0 + 1, :, xs], zn(3)))
    py = (same(hb.at[c, x, q0, :, ysl(y)], zn(1)), same(hb.at[c, x, q0 + 1, :, ysl(y)], zn(3)))
    z1 = [same(hb.at[c, x, zq(z), :, zs], xn(d)) for d in (1, 3, 2)]
    y1 = [same(hb.at[c, x, pl.ds(q0, 2), :, ysl(y)], xn(d)) for d in (1, 3, 2)]
    x1 = [same(hb.at[c, x, pl.ds(q0, 2), :, xs], xn(d)) for d in (1, 3, 2)]
    wx = send(w.at[o], ws, sib)
    arrive(*py)
    y2 = [same(hb.at[c, x, pl.ds(qo, 2), :, ysl(y)], xn(d)) for d in (1, 3, 2)]
    arrive(*px)
    x2 = [same(hb.at[c, x, pl.ds(qo, 2), :, xs], xn(d)) for d in (1, 3, 2)]
    dx0 = same(hb.at[c, x, pl.ds(qo, 2), :, xs], sib)
    arrive(*z1)
    z2 = [same(hb.at[c, :, zq(z), :, zs], zn(d)) for d in (1, 3, 2)]
    dz0 = same(hb.at[c, :, zq(z), :, zs], sib)
    arrive(*y1)
    arrive(*y2)
    y3 = [same(hb.at[c, :, :, :, ysl(y)], yn(d)) for d in (1, 3, 2)]
    dy0 = same(hb.at[c, :, :, :, ysl(y)], sib)

    def give(i, carry):
        t = lax.rem(me + i, 128)
        pltpu.make_async_remote_copy(
            src_ref=tea.at[t], dst_ref=rt.at[me], send_sem=tss, recv_sem=trs,
            device_id=(t // 16, lax.rem(t, 16)), device_id_type=MESH,
        ).start()
        return carry

    lax.fori_loop(1, 128, give, 0)

    acc[...] = jnp.zeros_like(acc)

    def mul_x(h, xx):
        lhs = hb[h, xx, :, :, xs].reshape(192, XW)
        rows = pl.ds(pl.multiple_of(192 * xx, 64), 192)
        acc[rows, :] += jnp.dot(lhs, wb[h, xs, :], preferred_element_type=F32)

    def mul_y(h, yy):
        lhs = hb[h, :, :, :, ysl(yy)].reshape(768, YW)
        acc[...] += jnp.dot(lhs, wb[h, ysl(yy), :], preferred_element_type=F32)

    def mul_z(h, zz):
        q = zq(zz)
        lhs = hb[h, :, q, :, zs].reshape(192, ZW)
        res = jnp.dot(lhs, wb[h, zs, :], preferred_element_type=F32)
        for xx in range(4):
            rows = pl.ds(pl.multiple_of(192 * xx + 48 * q, 16), 48)
            acc[rows, :] += res[48 * xx : 48 * xx + 48]

    for p in range(3):
        for a in range(6):
            i = lax.broadcasted_iota(jnp.int32, (128, 1), 0) + 128 * a
            n = (i * 43691) >> 19
            k = i - 12 * n
            core = jnp.where(k >= 6, 1, 0)
            first, second, third = n >> 4, (n >> 2) & 3, n & 3
            rx, ry, rz = ((first, second, third), (third, first, second), (second, third, first))[p]
            row = 6 * ((rx * 2 + (rz & 1)) * 16 + (rz >> 1) * 8 + ry * 2 + core) + k - 6 * core
            col = lax.broadcasted_iota(jnp.int32, (128, 768), 1)
            token = jnp.sum(jnp.where(col == row, tok[...], 0.0), axis=1, keepdims=True)
            perm[p, 128 * a : 128 * a + 128, :] = jnp.where(col.astype(F32) == token, 1.0, 0.0).astype(BF16)

    wcopy.wait()
    mul_x(c, x)
    mul_z(c, z)
    mul_y(c, y)
    other.wait()
    arrive(dx0)
    mul_x(o, x)
    arrive(dz0)
    mul_z(o, z)
    arrive(dy0)
    mul_y(o, y)
    dxs, dzs, dys = [], [], []
    for i, d in enumerate((3, 1, 2)):
        arrive(x1[i], x2[i])
        dxs.append(same(hb.at[c, rot(x, d), :, :, xs], sib))
        mul_x(c, rot(x, d))
    for i, d in enumerate((3, 1, 2)):
        arrive(z2[i])
        dzs.append(same(hb.at[c, :, zq(rot(z, d)), :, zs], sib))
        arrive(y3[i])
        dys.append(same(hb.at[c, :, :, :, ysl(rot(y, d))], sib))
        arrive(dxs[i])
        mul_x(o, rot(x, d))
        mul_z(c, rot(z, d))
        mul_y(c, rot(y, d))
        if i > 0:
            e = (3, 1, 2)[i - 1]
            arrive(dzs[i - 1])
            mul_z(o, rot(z, e))
            arrive(dys[i - 1])
            mul_y(o, rot(y, e))
    arrive(dzs[2])
    mul_z(o, rot(z, 2))
    arrive(dys[2])
    mul_y(o, rot(y, 2))

    eye = lax.broadcasted_iota(jnp.int32, (128, 128), 0) == lax.broadcasted_iota(jnp.int32, (128, 128), 1)
    st0[...] = jnp.zeros_like(st0)

    def to_row(v):
        return jnp.sum(jnp.where(eye, v, 0.0), axis=0, keepdims=True)

    def to_col(v):
        return jnp.sum(jnp.where(eye, v, 0.0), axis=1, keepdims=True)

    for a in range(6):
        rows = slice(128 * a, 128 * a + 128)
        l = acc[rows, :]
        m = jnp.max(l, axis=1, keepdims=True)
        e = jnp.exp(l - m)
        acc[rows, :] = e
        st0[a : a + 1, :] = to_row(m)
        st0[8 + a : 9 + a, :] = to_row(jnp.sum(e, axis=1, keepdims=True))

    def merge(first, ref, n):
        m = first[0:8]
        for k in range(1, n):
            m = jnp.maximum(m, ref[k, 0:8, :])
        s = first[8:16] * jnp.exp(first[0:8] - m)
        for k in range(1, n):
            s += ref[k, 8:16, :] * jnp.exp(ref[k, 0:8, :] - m)
        return m, s

    cps = []
    for d in range(4):
        for e in range(2):
            if d + e > 0:
                to = device(rot(x, d), y, z, c if e == 0 else o)
                cps.append(send(st0, st1.at[2 * d + e], to))
    arrive(*cps)
    m, s = merge(st0[...], st1, 8)
    st2[0, 0:8, :] = m
    st2[0, 8:16, :] = s
    cps = []
    for d in range(4):
        for e in range(4):
            if d + e > 0:
                cps.append(send(st2.at[0], st2.at[4 * d + e], device(x, rot(y, d), rot(z, e), c)))

    tcopy.wait()
    whole = pltpu.make_async_remote_copy(
        src_ref=tea.at[pl.ds(0, 127)], dst_ref=rt.at[pl.ds(0, 127)], send_sem=tss, recv_sem=trs,
        device_id=sib, device_id_type=MESH,
    )
    whole.wait_recv()
    i = lax.broadcasted_iota(jnp.int32, (240, 1), 0)
    j = (i * 1366) >> 16
    k = i - 48 * j
    t = (k * 43) >> 8
    want = t * 32 + j * 6 + (k - 6 * t)
    pick = jnp.where(lax.broadcasted_iota(jnp.int32, (240, 256), 1) == want, 1.0, 0.0).astype(BF16)

    def place(n, carry):
        src = rt[pl.ds(8 * n, 8)].reshape(256, 128)
        res = jnp.dot(pick, src, preferred_element_type=F32).astype(BF16)
        for jj in range(5):
            qb[pl.ds(pl.multiple_of(48 * n, 16), 48), 128 * jj : 128 * jj + 128] = res[48 * jj : 48 * jj + 48]
        return carry

    lax.fori_loop(0, 16, place, 0)

    arrive(*cps)
    m, s = merge(st2[0], st2, 16)
    scale = ups[...] * jnp.exp(st0[0:6, :] - m[0:6]) / s[0:6]
    for a in range(6):
        rows = slice(128 * a, 128 * a + 128)
        sc = to_col(scale[a : a + 1, :])
        uc = to_col(ups[a : a + 1, :])
        g[rows, :] = (acc[rows, :] * sc - uc * qb[rows, :].astype(F32)).astype(BF16)

    gsend = []
    for p in range(3):
        for a in range(3):
            rows = slice(256 * a, 256 * a + 256)
            gp[p, rows, :] = jnp.dot(perm[p, rows, :], g[...], preferred_element_type=F32).astype(BF16)
        gsend.append(send(gp.at[p], gs.at[p], sib))
    wx.wait_recv()

    co = (x, y, z)
    near = (xn, yn, zn)
    nt = (((1,), (1,)), ((), ()))
    sa, sb, sc3 = {}, {}, {}

    def head_part(n):
        h, k = n // 5, n % 5
        lhs = hb[h, :, :, :, 512 * k : 512 * k + 512].reshape(768, 512)
        res = lax.dot_general(lhs, g[...], (((0,), (0,)), ((), ())), preferred_element_type=F32)
        ghb[512 * n : 512 * n + 512, :] = res.astype(BF16)
        cp = pltpu.make_async_copy(ghb.at[pl.ds(512 * n, 512)], gh.at[pl.ds(512 * n, 512)], ls.at[4 + n])
        cp.start()
        return cp

    def stage_a(p, k):
        start, widths = LANES[p]
        wd = widths[k]
        at = start + (widths[0] if k else 0)
        wo = wb[c, at : at + wd, :]
        wt = ws[at : at + wd, :]
        for a in range(4):
            rows = slice(192 * a, 192 * a + 192)
            res = lax.dot_general(gp[p, rows, :], wo, nt, preferred_element_type=F32)
            res += lax.dot_general(gs[p, rows, :], wt, nt, preferred_element_type=F32)
            tps[p][k][a] = res.astype(BF16)
        sa[p, k] = [send(tps[p][k].at[rot(co[p], d)], ras[p][k].at[d - 1], near[p](d)) for d in (1, 3, 2)]

    def stage_b(p, k):
        ax = (p + 1) % 3
        arrive(*sa[p, k])
        ra = ras[p][k]
        res = tps[p][k][co[p]].astype(F32) + ra[0].astype(F32) + ra[1].astype(F32) + ra[2].astype(F32)
        res = res.astype(BF16)
        for a in range(4):
            tbs[p][k][a] = res[48 * a : 48 * a + 48]
        sb[p, k] = [send(tbs[p][k].at[rot(co[ax], d)], rbs[p][k].at[d - 1], near[ax](d)) for d in (1, 3, 2)]

    def window(i):
        return pl.ds(pl.multiple_of(8 * (i + i // 2), 8), 16)

    def stage_c(p, k):
        ax, ay = (p + 1) % 3, (p + 2) % 3
        arrive(*sb[p, k])
        rb = rbs[p][k]
        tcs[p][k][...] = tbs[p][k][co[ax]].astype(F32) + rb[0].astype(F32) + rb[1].astype(F32) + rb[2].astype(F32)
        sc3[p, k] = [
            send(tcs[p][k].at[window(rot(co[ay], d))], rcs[p][k].at[d - 1], near[ay](d)) for d in (1, 3, 2)]

    def stage_d(p, k):
        start, widths = LANES[p]
        at = start + (widths[0] if k else 0)
        arrive(*sc3[p, k])
        rc = rcs[p][k]
        fin[:, at : at + widths[k]] = tcs[p][k][window(co[(p + 2) % 3]), :] + rc[0] + rc[1] + rc[2]

    heads = []
    for k in range(2):
        for p in range(3):
            if k == 0:
                arrive(gsend[p])
            stage_a(p, k)
    for n in range(4):
        heads.append(head_part(n))
    for p in range(3):
        stage_b(p, 0)
    for n in range(4, 8):
        heads.append(head_part(n))
    for p in range(3):
        stage_c(p, 0)
    for p in range(3):
        stage_b(p, 1)
    for n in range(8, 10):
        heads.append(head_part(n))
    for p in range(3):
        stage_d(p, 0)
    for p in range(3):
        stage_c(p, 1)
    for p in range(3):
        stage_d(p, 1)
    arrive(send(fin, fs, sib))
    for p in range(3):
        start, widths = LANES[p]
        wd = widths[0] + widths[1]
        odd = lax.rem(co[(p + 2) % 3], 2)
        cols = slice(start, start + wd)
        mine, theirs = fin[:, cols], fs[:, cols]

        def rows_of(v):
            even_rows = jnp.where(c == 0, v[0:6], v[6:12])
            odd_rows = jnp.where(c == 0, v[4:10], v[10:16])
            return jnp.where(odd == 0, even_rows, odd_rows).astype(BF16)

        lo = jnp.where(c == 0, mine, theirs)
        hi = jnp.where(c == 0, theirs, mine)
        gx[:, start : start + wd] = rows_of(lo)
        gx[:, HALF + start : HALF + start + wd] = rows_of(hi)

    for cp in heads:
        cp.wait()
    for cp in sent:
        cp.wait_send()
    whole.wait_send()


def shards(hidden_rows, head_weight, teacher_logits, upstream, block_map, token_order):
    vmem = pl.BlockSpec(memory_space=pltpu.VMEM)
    anyw = pl.BlockSpec(memory_space=pl.ANY)
    probs = pl.pallas_call(
        teacher_kernel,
        out_shape=jax.ShapeDtypeStruct((128, 32, 128), BF16),
        in_specs=[pl.BlockSpec(memory_space=pltpu.SMEM), vmem],
        out_specs=vmem,
        compiler_params=pltpu.CompilerParams(vmem_limit_bytes=32 << 20),
        name="teacher_probs",
    )(block_map, teacher_logits)

    def per_unit(shape, dtype):
        return [pltpu.VMEM(shape(wd), dtype) for _, widths in LANES for wd in widths]

    scratch = [
        pltpu.VMEM((2, 4, 4, 48, HALF), BF16),
        pltpu.VMEM((2, HALF, 640), BF16),
        pltpu.VMEM((HALF, 640), BF16),
        pltpu.VMEM((768, 640), F32),
        pltpu.VMEM((768, 640), BF16),
        pltpu.VMEM((128, 32, 128), BF16),
        pltpu.VMEM((768, 640), BF16),
        pltpu.VMEM((16, 128), F32),
        pltpu.VMEM((8, 16, 128), F32),
        pltpu.VMEM((16, 16, 128), F32),
        pltpu.VMEM((3, 768, 768), BF16),
        pltpu.VMEM((3, 768, 640), BF16),
        pltpu.VMEM((3, 768, 640), BF16),
        pltpu.VMEM((5120, 640), BF16),
        pltpu.VMEM((16, HALF), F32),
        pltpu.VMEM((16, HALF), F32),
        *per_unit(lambda wd: (4, 192, wd), BF16),
        *per_unit(lambda wd: (3, 192, wd), BF16),
        *per_unit(lambda wd: (4, 48, wd), BF16),
        *per_unit(lambda wd: (3, 48, wd), BF16),
        *per_unit(lambda wd: (48, wd), F32),
        *per_unit(lambda wd: (3, 16, wd), F32),
        pltpu.SemaphoreType.DMA((128,)),
        pltpu.SemaphoreType.DMA((128,)),
        pltpu.SemaphoreType.DMA((16,)),
        pltpu.SemaphoreType.DMA,
        pltpu.SemaphoreType.DMA,
    ]
    return pl.pallas_call(
        head_kernel,
        out_shape=(jax.ShapeDtypeStruct((5120, 640), BF16), jax.ShapeDtypeStruct((6, 5120), BF16)),
        in_specs=[anyw, anyw, anyw, vmem, vmem],
        out_specs=(anyw, vmem),
        scratch_shapes=scratch,
        compiler_params=pltpu.CompilerParams(
            collective_id=0, has_side_effects=True, vmem_limit_bytes=62 << 20),
        name="head_backward",
    )(
        hidden_rows.reshape(2, 48, 5120),
        head_weight.reshape(2, HALF, 640),
        probs,
        upstream.reshape(6, 128),
        token_order.astype(F32).reshape(1, 768),
    )


def solution(mesh):
    in_specs = (P("dp", None), P(None, ("dp", "vocab")), P(("dp", "vocab"), None), P(), P(), P())
    out_specs = (P(None, ("dp", "vocab")), P(("dp", "vocab"), None))
    return jax.shard_map(shards, mesh=mesh, in_specs=in_specs, out_specs=out_specs, check_vma=False)
```

```python
import jax
import jax.numpy as jnp
from jax import lax
from jax.experimental import pallas as pl
from jax.experimental.pallas import tpu as pltpu
from jax.sharding import PartitionSpec as P

MESH = pl.DeviceIdType.MESH
F32 = jnp.float32
BF16 = jnp.bfloat16
HALF = 2560
XW, YW, ZW = 512, 256, 1024
Y0, Z0 = 512, 1536
LANES = ((0, (512, 384)), (896, (512, 384)), (1792, (384, 384)))


def device(x, y, z, c):
    return (x * 2 + lax.rem(z, 2), (z // 2) * 8 + y * 2 + c)


def head_kernel(
    hid, w, tea, bmap, ups, tok, gh, gx,
    hb, wb, ws, acc, qb, rt, tv, mt, g, st0, st1, st2, perm, gp, gs, ghb, fin, fs,
    t00, t01, t10, t11, t20, t21, a00, a01, a10, a11, a20, a21,
    u00, u01, u10, u11, u20, u21, b00, b01, b10, b11, b20, b21,
    v00, v01, v10, v11, v20, v21, c00, c01, c10, c11, c20, c21,
    ss, rs, ls, tss, trs, hx, hy, hc,
):
    tps = ((t00, t01), (t10, t11), (t20, t21))
    ras = ((a00, a01), (a10, a11), (a20, a21))
    tbs = ((u00, u01), (u10, u11), (u20, u21))
    rbs = ((b00, b01), (b10, b11), (b20, b21))
    tcs = ((v00, v01), (v10, v11), (v20, v21))
    rcs = ((c00, c01), (c10, c11), (c20, c21))
    dp = lax.axis_index("dp")
    vo = lax.axis_index("vocab")
    x, zl = dp // 2, lax.rem(dp, 2)
    zh, y, c = vo // 8, lax.rem(vo // 2, 4), lax.rem(vo, 2)
    z = zh * 2 + zl
    o = 1 - c
    me = dp * 16 + vo

    def rot(v, d):
        return lax.rem(v + d, 4)

    def xn(d):
        return device(rot(x, d), y, z, c)

    def yn(d):
        return device(x, rot(y, d), z, c)

    def zn(d):
        return device(x, y, rot(z, d), c)

    sib = device(x, y, z, o)
    sent = []

    def send(src, dst, to):
        k = len(sent)
        cp = pltpu.make_async_remote_copy(
            src_ref=src, dst_ref=dst, send_sem=ss.at[k], recv_sem=rs.at[k],
            device_id=to, device_id_type=MESH,
        )
        cp.start()
        sent.append(cp)
        return cp

    def arrive(*cps):
        for cp in cps:
            cp.wait_recv()

    q0, qo = 2 * zl, 2 * (1 - zl)
    mine = pl.multiple_of(HALF * c, 128)
    own = (
        pltpu.make_async_copy(hid.at[:, :, pl.ds(mine, XW)], hb.at[c, x, pl.ds(q0, 2), :, pl.ds(0, XW)], ls.at[0]),
        pltpu.make_async_copy(
            hid.at[:, :, pl.ds(pl.multiple_of(mine + Y0 + YW * y, 128), YW)],
            hb.at[c, x, pl.ds(q0, 2), :, pl.ds(pl.multiple_of(Y0 + YW * y, 128), YW)], ls.at[14]),
        pltpu.make_async_copy(
            hid.at[zh, :, pl.ds(pl.multiple_of(mine + Z0, 128), ZW)],
            hb.at[c, x, q0 + zh, :, pl.ds(Z0, ZW)], ls.at[15]),
    )
    for cp in own:
        cp.start()
    other = pltpu.make_async_copy(
        hid.at[:, :, pl.ds(pl.multiple_of(HALF * o, 128), XW)],
        hb.at[o, x, pl.ds(q0, 2), :, pl.ds(0, XW)], ls.at[1])
    other.start()
    wcopy = pltpu.make_async_copy(w, wb, ls.at[2])
    wcopy.start()
    def fetch(j, carry):
        cols = pl.ds(pl.multiple_of(j * HALF, 128), HALF)
        pltpu.make_async_copy(tea.at[:, cols], tv.at[j], ls.at[3]).start()
        return carry

    lax.fori_loop(0, 32, fetch, 0)
    tcopy = pltpu.make_async_copy(tv, tv, ls.at[3])

    bar = pltpu.get_barrier_semaphore()

    peers = [f(d) for f in (xn, yn, zn) for d in (1, 3, 2)] + [sib]
    for to in peers:
        pl.semaphore_signal(bar, inc=1, device_id=to, device_id_type=MESH)
    pl.semaphore_wait(bar, len(peers))
    for cp in own:
        cp.wait()

    def ysl(yy):
        return pl.ds(pl.multiple_of(Y0 + YW * yy, 128), YW)

    def zq(zz):
        return 2 * lax.rem(zz, 2) + zz // 2

    def same(ref, to):
        return send(ref, ref, to)

    xs, zs = pl.ds(0, XW), pl.ds(Z0, ZW)
    za, zb = pl.ds(Z0, ZW // 2), pl.ds(Z0 + ZW // 2, ZW // 2)

    def greet(sem, to):
        for dev in to:
            pl.semaphore_signal(sem, inc=1, device_id=dev, device_id_type=MESH)

    def fold(v, op):
        r = v[:, 0:128]
        for n in range(1, 20):
            r = op(r, v[:, 128 * n : 128 * n + 128])
        return r

    def tea_cols(j):
        return tv[j].astype(F32)

    def tea_max():
        top = lax.fori_loop(
            0, 32, lambda j, m: jnp.maximum(m, fold(tea_cols(j), jnp.maximum)), jnp.full((6, 128), -jnp.inf, F32))
        return jnp.max(top, axis=1, keepdims=True)

    def tea_sum(m):
        tot = lax.fori_loop(
            0, 32, lambda j, s: s + fold(jnp.exp(tea_cols(j) - m), jnp.add), jnp.zeros((6, 128), F32))
        return jnp.sum(tot, axis=1, keepdims=True)

    def tea_write(m, s, lo, hi):
        inv = 1.0 / s
        pad = jnp.zeros((2, 128), F32)

        def block(j, carry):
            p = jnp.exp(tea_cols(bmap[j]) - m) * inv
            for n in range(4):
                rows = [p[:, 640 * n + 128 * i : 640 * n + 128 * i + 128] for i in range(5)]
                mt[4 * j + n] = jnp.concatenate(rows + [pad], axis=0).astype(BF16)
            return carry

        lax.fori_loop(lo, hi, block, 0)

    def give(lo, hi):
        def one(i, carry):
            t = lax.rem(me + i, 128)
            pltpu.make_async_remote_copy(
                src_ref=mt.at[t], dst_ref=rt.at[me], send_sem=tss, recv_sem=trs,
                device_id=(lax.div(t, 16), lax.rem(t, 16)), device_id_type=MESH,
            ).start()
            return carry

        lax.fori_loop(lo, hi, one, 0)

    class Ring:
        def __init__(self, near, at, part, half, own_to_sib=True):
            self.near, self.at, self.part, self.half, self.own_to_sib = near, at, part, half, own_to_sib

        def start(self):
            ref = self.part(self.at)
            self.right, self.left = same(ref, self.near(1)), same(ref, self.near(3))
            self.own = same(ref, sib) if self.own_to_sib else None

        def forward(self):
            before, after = rot(self.at, 3), rot(self.at, 1)
            arrive(self.right)
            self.far = [same(self.half(before, 0), self.near(1))]
            arrive(self.left)
            self.far.append(same(self.half(after, 1), self.near(3)))
            self.sides = [same(self.part(before), sib), same(self.part(after), sib)]

        def finish(self):
            arrive(*self.far)
            self.end = same(self.part(rot(self.at, 2)), sib)

    def xring(q, own_to_sib):
        return Ring(
            xn, x, lambda v: hb.at[c, v, pl.ds(q, 2), :, xs], lambda v, i: hb.at[c, v, q + i, :, xs], own_to_sib)

    def yring(q):
        return Ring(
            yn, y, lambda v: hb.at[c, :, pl.ds(q, 2), :, ysl(v)],
            lambda v, i: hb.at[c, pl.ds(2 * i, 2), pl.ds(q, 2), :, ysl(v)])

    def zring(cols):
        return Ring(
            zn, z, lambda v: hb.at[c, :, zq(v), :, cols], lambda v, i: hb.at[c, pl.ds(2 * i, 2), zq(v), :, cols])

    xra, xrb = xring(q0, False), xring(qo, True)
    yra, yrb = yring(q0), yring(qo)
    zra, zrb = zring(za), zring(zb)

    def mul_x(h, xx):
        lhs = hb[h, xx, :, :, xs].reshape(192, XW)
        rows = pl.ds(pl.multiple_of(192 * xx, 64), 192)
        acc[rows, :] += jnp.dot(lhs, wb[h, xs, :], preferred_element_type=F32)

    def mul_y(h, yy):
        lhs = hb[h, :, :, :, ysl(yy)].reshape(768, YW)
        acc[...] += jnp.dot(lhs, wb[h, ysl(yy), :], preferred_element_type=F32)

    def mul_z(h, zz):
        q = zq(zz)
        lhs = hb[h, :, q, :, zs].reshape(192, ZW)
        res = jnp.dot(lhs, wb[h, zs, :], preferred_element_type=F32)
        for xx in range(4):
            rows = pl.ds(pl.multiple_of(192 * xx + 48 * q, 16), 48)
            acc[rows, :] += res[48 * xx : 48 * xx + 48]

    def make_perm(p):
        for a in range(6):
            i = lax.broadcasted_iota(jnp.int32, (128, 1), 0) + 128 * a
            n = (i * 43691) >> 19
            k = i - 12 * n
            core = jnp.where(k >= 6, 1, 0)
            first, second, third = n >> 4, (n >> 2) & 3, n & 3
            rx, ry, rz = ((first, second, third), (third, first, second), (second, third, first))[p]
            row = 6 * ((rx * 2 + (rz & 1)) * 16 + (rz >> 1) * 8 + ry * 2 + core) + k - 6 * core
            lane = lax.broadcasted_iota(jnp.int32, (128, 128), 1)
            token = jnp.zeros((128, 128), F32)
            for b in range(6):
                token += jnp.where(lane == row - 128 * b, tok[b : b + 1, :].astype(F32), 0.0)
            token = jnp.sum(token, axis=1, keepdims=True)
            col = lax.broadcasted_iota(jnp.int32, (128, 768), 1)
            perm[p, 128 * a : 128 * a + 128, :] = jnp.where(col.astype(F32) == token, 1.0, 0.0).astype(BF16)

    own2, two = pl.ds(q0, 2), pl.ds(qo, 2)
    y1 = [same(hb.at[c, x, own2, :, ysl(y)], xn(d)) for d in (1, 3, 2)]
    py = (same(hb.at[c, x, q0, :, ysl(y)], zn(1)), same(hb.at[c, x, q0 + 1, :, ysl(y)], zn(3)))
    za1 = [same(hb.at[c, x, zq(z), :, za], xn(d)) for d in (1, 3, 2)]
    px = (same(hb.at[c, x, q0, :, xs], zn(1)), same(hb.at[c, x, q0 + 1, :, xs], zn(3)))
    greet(hx, [xn(d) for d in (1, 3, 2)])
    wx = send(w.at[o], ws, sib)
    tcopy.wait()
    tm = tea_max()
    arrive(*py)
    y2 = [same(hb.at[c, x, two, :, ysl(y)], xn(d)) for d in (1, 3, 2)]
    zb1 = [same(hb.at[c, x, zq(z), :, zb], xn(d)) for d in (1, 3, 2)]
    pl.semaphore_wait(hx, 3)
    greet(hy, [yn(d) for d in (1, 3, 2)])
    arrive(*y1)
    yra.start()
    arrive(*za1)
    zra.start()
    xra.start()
    ts = tea_sum(tm)
    pl.semaphore_wait(hy, 3)
    greet(hc, [sib])
    arrive(*px)
    xrb.start()
    tea_write(tm, ts, 0, 16)
    arrive(*y2)
    yrb.start()
    arrive(*zb1)
    zrb.start()
    tea_write(tm, ts, 16, 32)
    pl.semaphore_wait(hc, 1)
    rt[me] = mt[me]
    yra.forward()
    give(1, 17)
    zra.forward()
    give(17, 33)
    xra.forward()
    wcopy.wait()
    acc[...] = jnp.zeros_like(acc)
    mul_x(c, x)
    give(33, 49)
    mul_z(c, z)
    xrb.forward()
    give(49, 65)
    yrb.forward()
    give(65, 81)
    zrb.forward()
    give(81, 97)
    mul_y(c, y)
    give(97, 113)
    other.wait()
    arrive(xrb.own)
    mul_x(o, x)
    give(113, 128)
    arrive(zra.own, zrb.own)
    mul_z(o, z)
    arrive(yra.own, yrb.own)
    mul_y(o, y)
    for p in range(3):
        make_perm(p)
    for d in (3, 1):
        mul_x(c, rot(x, d))
        mul_y(c, rot(y, d))
        mul_z(c, rot(z, d))
    xra.finish()
    xrb.finish()
    mul_x(c, rot(x, 2))
    yra.finish()
    zra.finish()
    for i, d in enumerate((3, 1)):
        arrive(xra.sides[i], xrb.sides[i])
        mul_x(o, rot(x, d))
        arrive(yra.sides[i], yrb.sides[i])
        mul_y(o, rot(y, d))
        arrive(zra.sides[i], zrb.sides[i])
        mul_z(o, rot(z, d))
    yrb.finish()
    zrb.finish()
    mul_y(c, rot(y, 2))
    mul_z(c, rot(z, 2))
    arrive(xra.end, xrb.end)
    mul_x(o, rot(x, 2))
    arrive(yra.end, yrb.end)
    mul_y(o, rot(y, 2))
    arrive(zra.end, zrb.end)
    mul_z(o, rot(z, 2))

    eye = lax.broadcasted_iota(jnp.int32, (128, 128), 0) == lax.broadcasted_iota(jnp.int32, (128, 128), 1)
    st0[...] = jnp.zeros_like(st0)

    def to_row(v):
        return jnp.sum(jnp.where(eye, v, 0.0), axis=0, keepdims=True)

    def to_col(v):
        return jnp.sum(jnp.where(eye, v, 0.0), axis=1, keepdims=True)

    for a in range(6):
        rows = slice(128 * a, 128 * a + 128)
        l = acc[rows, :]
        m = jnp.max(l, axis=1, keepdims=True)
        e = jnp.exp(l - m)
        acc[rows, :] = e
        st0[a : a + 1, :] = to_row(m)
        st0[8 + a : 9 + a, :] = to_row(jnp.sum(e, axis=1, keepdims=True))

    def merge(first, ref, n):
        m = first[0:8]
        for k in range(1, n):
            m = jnp.maximum(m, ref[k, 0:8, :])
        s = first[8:16] * jnp.exp(first[0:8] - m)
        for k in range(1, n):
            s += ref[k, 8:16, :] * jnp.exp(ref[k, 0:8, :] - m)
        return m, s

    cps = []
    for d in range(4):
        for e in range(2):
            if d + e > 0:
                to = device(rot(x, d), y, z, c if e == 0 else o)
                cps.append(send(st0, st1.at[2 * d + e], to))
    arrive(*cps)
    m, s = merge(st0[...], st1, 8)
    st2[0, 0:8, :] = m
    st2[0, 8:16, :] = s
    cps = []
    for d in range(4):
        for e in range(4):
            if d + e > 0:
                cps.append(send(st2.at[0], st2.at[4 * d + e], device(x, rot(y, d), rot(z, e), c)))

    whole = pltpu.make_async_remote_copy(
        src_ref=mt.at[pl.ds(0, 127)], dst_ref=rt.at[pl.ds(0, 127)], send_sem=tss, recv_sem=trs,
        device_id=sib, device_id_type=MESH,
    )
    whole.wait_recv()
    i = lax.broadcasted_iota(jnp.int32, (240, 1), 0)
    j = (i * 1366) >> 16
    k = i - 48 * j
    t = (k * 43) >> 8
    want = t * 32 + j * 6 + (k - 6 * t)
    pick = jnp.where(lax.broadcasted_iota(jnp.int32, (240, 256), 1) == want, 1.0, 0.0).astype(BF16)

    def place(n, carry):
        src = rt[pl.ds(8 * n, 8)].reshape(256, 128)
        res = jnp.dot(pick, src, preferred_element_type=F32).astype(BF16)
        for jj in range(5):
            qb[pl.ds(pl.multiple_of(48 * n, 16), 48), 128 * jj : 128 * jj + 128] = res[48 * jj : 48 * jj + 48]
        return carry

    lax.fori_loop(0, 16, place, 0)

    arrive(*cps)
    m, s = merge(st2[0], st2, 16)
    scale = ups[...] * jnp.exp(st0[0:6, :] - m[0:6]) / s[0:6]
    for a in range(6):
        rows = slice(128 * a, 128 * a + 128)
        sc = to_col(scale[a : a + 1, :])
        uc = to_col(ups[a : a + 1, :])
        g[rows, :] = (acc[rows, :] * sc - uc * qb[rows, :].astype(F32)).astype(BF16)

    gsend = []
    for p in range(3):
        for a in range(3):
            rows = slice(256 * a, 256 * a + 256)
            gp[p, rows, :] = jnp.dot(perm[p, rows, :], g[...], preferred_element_type=F32).astype(BF16)
        gsend.append(send(gp.at[p], gs.at[p], sib))
    arrive(wx)

    co = (x, y, z)
    near = (xn, yn, zn)
    nt = (((1,), (1,)), ((), ()))
    sa, sb, sc3 = {}, {}, {}

    def head_part(n):
        h, k = n // 5, n % 5
        lhs = hb[h, :, :, :, 512 * k : 512 * k + 512].reshape(768, 512)
        res = lax.dot_general(lhs, g[...], (((0,), (0,)), ((), ())), preferred_element_type=F32)
        ghb[512 * n : 512 * n + 512, :] = res.astype(BF16)
        cp = pltpu.make_async_copy(ghb.at[pl.ds(512 * n, 512)], gh.at[pl.ds(512 * n, 512)], ls.at[4 + n])
        cp.start()
        return cp

    def stage_a(p, k):
        start, widths = LANES[p]
        wd = widths[k]
        at = start + (widths[0] if k else 0)
        wo = wb[c, at : at + wd, :]
        wt = ws[at : at + wd, :]
        tp, ra, v = tps[p][k], ras[p][k], co[p]
        on, back = ((1, 3), (3, 1))[k]
        sa[p, k] = []
        for d in (2, back, on, 0):
            a = rot(v, d)
            rows = pl.ds(pl.multiple_of(192 * a, 64), 192)
            res = lax.dot_general(gp[p, rows, :], wo, nt, preferred_element_type=F32)
            res += lax.dot_general(gs[p, rows, :], wt, nt, preferred_element_type=F32)
            tp[a] = res.astype(BF16)
            if d == 2:
                sa[p, k].append(send(tp.at[a], ra.at[2], near[p](on)))
            if d == back:
                sa[p, k].append(send(tp.at[a], ra.at[0], near[p](back)))

    def pass_a(p, k):
        tp, ra, on = tps[p][k], ras[p][k], (1, 3)[k]
        arrive(sa[p, k][0])
        a = rot(co[p], on)
        tp[a] = (tp[a].astype(F32) + ra[2].astype(F32)).astype(BF16)
        sa[p, k].append(send(tp.at[a], ra.at[1], near[p](on)))

    def stage_b(p, k):
        ax = (p + 1) % 3
        arrive(*sa[p, k][1:])
        ra = ras[p][k]
        res = tps[p][k][co[p]].astype(F32) + ra[0].astype(F32) + ra[1].astype(F32)
        res = res.astype(BF16)
        for a in range(4):
            tbs[p][k][a] = res[48 * a : 48 * a + 48]
        sb[p, k] = [send(tbs[p][k].at[rot(co[ax], d)], rbs[p][k].at[d - 1], near[ax](d)) for d in (1, 3, 2)]

    def window(i):
        return pl.ds(pl.multiple_of(8 * (i + i // 2), 8), 16)

    def stage_c(p, k):
        ax, ay = (p + 1) % 3, (p + 2) % 3
        arrive(*sb[p, k])
        rb = rbs[p][k]
        tcs[p][k][...] = tbs[p][k][co[ax]].astype(F32) + rb[0].astype(F32) + rb[1].astype(F32) + rb[2].astype(F32)
        sc3[p, k] = [
            send(tcs[p][k].at[window(rot(co[ay], d))], rcs[p][k].at[d - 1], near[ay](d)) for d in (1, 3, 2)]

    def stage_d(p, k):
        start, widths = LANES[p]
        at = start + (widths[0] if k else 0)
        arrive(*sc3[p, k])
        rc = rcs[p][k]
        fin[:, at : at + widths[k]] = tcs[p][k][window(co[(p + 2) % 3]), :] + rc[0] + rc[1] + rc[2]

    heads = []
    for p in range(3):
        arrive(gsend[p])
        stage_a(p, 0)
    for p in range(3):
        stage_a(p, 1)
        pass_a(p, 0)
    for n in range(2):
        heads.append(head_part(n))
    for p in range(3):
        pass_a(p, 1)
    for n in range(2, 5):
        heads.append(head_part(n))
    for p in range(3):
        stage_b(p, 0)
    for n in range(5, 8):
        heads.append(head_part(n))
    for p in range(3):
        stage_b(p, 1)
    for p in range(3):
        stage_c(p, 0)
    for n in range(8, 10):
        heads.append(head_part(n))
    for p in range(3):
        stage_d(p, 0)
    for p in range(3):
        stage_c(p, 1)
    for p in range(3):
        stage_d(p, 1)
    arrive(send(fin, fs, sib))
    for p in range(3):
        start, widths = LANES[p]
        wd = widths[0] + widths[1]
        odd = lax.rem(co[(p + 2) % 3], 2)
        cols = slice(start, start + wd)
        mine, theirs = fin[:, cols], fs[:, cols]

        def rows_of(v):
            even_rows = jnp.where(c == 0, v[0:6], v[6:12])
            odd_rows = jnp.where(c == 0, v[4:10], v[10:16])
            return jnp.where(odd == 0, even_rows, odd_rows).astype(BF16)

        lo = jnp.where(c == 0, mine, theirs)
        hi = jnp.where(c == 0, theirs, mine)
        gx[:, start : start + wd] = rows_of(lo)
        gx[:, HALF + start : HALF + start + wd] = rows_of(hi)

    for cp in heads:
        cp.wait()
    for cp in sent:
        cp.wait_send()
    whole.wait_send()


def shards(hidden_rows, head_weight, teacher_logits, upstream, block_map, token_order):
    vmem = pl.BlockSpec(memory_space=pltpu.VMEM)
    anyw = pl.BlockSpec(memory_space=pl.ANY)
    def per_unit(shape, dtype):
        return [pltpu.VMEM(shape(wd), dtype) for _, widths in LANES for wd in widths]

    scratch = [
        pltpu.VMEM((2, 4, 4, 48, HALF), BF16),
        pltpu.VMEM((2, HALF, 640), BF16),
        pltpu.VMEM((HALF, 640), BF16),
        pltpu.VMEM((768, 640), F32),
        pltpu.VMEM((768, 640), BF16),
        pltpu.VMEM((128, 32, 128), BF16),
        pltpu.VMEM((32, 6, HALF), BF16),
        pltpu.VMEM((128, 32, 128), BF16),
        pltpu.VMEM((768, 640), BF16),
        pltpu.VMEM((16, 128), F32),
        pltpu.VMEM((8, 16, 128), F32),
        pltpu.VMEM((16, 16, 128), F32),
        pltpu.VMEM((3, 768, 768), BF16),
        pltpu.VMEM((3, 768, 640), BF16),
        pltpu.VMEM((3, 768, 640), BF16),
        pltpu.VMEM((5120, 640), BF16),
        pltpu.VMEM((16, HALF), F32),
        pltpu.VMEM((16, HALF), F32),
        *per_unit(lambda wd: (4, 192, wd), BF16),
        *per_unit(lambda wd: (3, 192, wd), BF16),
        *per_unit(lambda wd: (4, 48, wd), BF16),
        *per_unit(lambda wd: (3, 48, wd), BF16),
        *per_unit(lambda wd: (48, wd), F32),
        *per_unit(lambda wd: (3, 16, wd), F32),
        pltpu.SemaphoreType.DMA((160,)),
        pltpu.SemaphoreType.DMA((160,)),
        pltpu.SemaphoreType.DMA((16,)),
        pltpu.SemaphoreType.DMA,
        pltpu.SemaphoreType.DMA,
        pltpu.SemaphoreType.REGULAR,
        pltpu.SemaphoreType.REGULAR,
        pltpu.SemaphoreType.REGULAR,
    ]
    return pl.pallas_call(
        head_kernel,
        out_shape=(jax.ShapeDtypeStruct((5120, 640), BF16), jax.ShapeDtypeStruct((6, 5120), BF16)),
        in_specs=[anyw, anyw, anyw, pl.BlockSpec(memory_space=pltpu.SMEM), vmem, vmem],
        out_specs=(anyw, vmem),
        scratch_shapes=scratch,
        compiler_params=pltpu.CompilerParams(
            collective_id=0, has_side_effects=True, vmem_limit_bytes=62 << 20),
        name="head_backward",
    )(
        hidden_rows.reshape(2, 48, 5120),
        head_weight.reshape(2, HALF, 640),
        teacher_logits,
        block_map,
        upstream.reshape(6, 128),
        token_order.reshape(6, 128),
    )


def solution(mesh):
    in_specs = (P("dp", None), P(None, ("dp", "vocab")), P(("dp", "vocab"), None), P(), P(), P())
    out_specs = (P(None, ("dp", "vocab")), P(("dp", "vocab"), None))
    return jax.shard_map(shards, mesh=mesh, in_specs=in_specs, out_specs=out_specs, check_vma=False)
```

```python
import jax
import jax.numpy as jnp
from jax import lax
from jax.experimental import pallas as pl
from jax.experimental.pallas import tpu as pltpu
from jax.sharding import PartitionSpec as P

MESH = pl.DeviceIdType.MESH
F32 = jnp.float32
BF16 = jnp.bfloat16
HALF = 2560
XW, YW, ZW = 512, 256, 1024
Y0, Z0 = 512, 1536
UNITS = (((0, 512), (512, 256)), ((768, 512), (1280, 256)), ((1536, 512), (2048, 512)))
AXES = ((0, 1, 2), (1, 0, 2), (2, 0, 1))


def device(x, y, z, c):
    return (x * 2 + lax.rem(z, 2), (z // 2) * 8 + y * 2 + c)


def head_kernel(
    hid, w, tea, bmap, ups, tok, gh, gx,
    hb, wb, wc, acc, qb, rr, rt, tv, mt, g, st0, st1, st2, perm, gc, ghb, fin, fs,
    t00, t01, t10, t11, t20, t21, a00, a01, a10, a11, a20, a21,
    u00, u01, u10, u11, u20, u21, b00, b01, b10, b11, b20, b21,
    v00, v01, v10, v11, v20, v21, c00, c01, c10, c11, c20, c21,
    ss, rs, ls, tss, trs, hx, hy,
):
    tps = ((t00, t01), (t10, t11), (t20, t21))
    ras = ((a00, a01), (a10, a11), (a20, a21))
    tbs = ((u00, u01), (u10, u11), (u20, u21))
    rbs = ((b00, b01), (b10, b11), (b20, b21))
    tcs = ((v00, v01), (v10, v11), (v20, v21))
    rcs = ((c00, c01), (c10, c11), (c20, c21))
    dp = lax.axis_index("dp")
    vo = lax.axis_index("vocab")
    x, zl = dp // 2, lax.rem(dp, 2)
    zh, y, c = vo // 8, lax.rem(vo // 2, 4), lax.rem(vo, 2)
    z = zh * 2 + zl
    o = 1 - c
    me = dp * 16 + vo

    def rot(v, d):
        return lax.rem(v + d, 4)

    def xn(d):
        return device(rot(x, d), y, z, c)

    def yn(d):
        return device(x, rot(y, d), z, c)

    def zn(d):
        return device(x, y, rot(z, d), c)

    sib = device(x, y, z, o)
    sent = []

    def send(src, dst, to):
        k = len(sent)
        cp = pltpu.make_async_remote_copy(
            src_ref=src, dst_ref=dst, send_sem=ss.at[k], recv_sem=rs.at[k],
            device_id=to, device_id_type=MESH,
        )
        cp.start()
        sent.append(cp)
        return cp

    def arrive(*cps):
        for cp in cps:
            cp.wait_recv()

    bar = pltpu.get_barrier_semaphore()

    peers = [f(d) for f in (xn, yn, zn) for d in (1, 3, 2)] + [sib]
    for to in peers:
        pl.semaphore_signal(bar, inc=1, device_id=to, device_id_type=MESH)
    q0, qo = 2 * zl, 2 * (1 - zl)
    mine = pl.multiple_of(HALF * c, 128)
    own = (
        pltpu.make_async_copy(hid.at[:, :, pl.ds(mine, XW)], hb.at[c, x, pl.ds(q0, 2), :, pl.ds(0, XW)], ls.at[0]),
        pltpu.make_async_copy(
            hid.at[:, :, pl.ds(pl.multiple_of(mine + Y0 + YW * y, 128), YW)],
            hb.at[c, x, pl.ds(q0, 2), :, pl.ds(pl.multiple_of(Y0 + YW * y, 128), YW)], ls.at[14]),
        pltpu.make_async_copy(
            hid.at[zh, :, pl.ds(pl.multiple_of(mine + Z0, 128), ZW)],
            hb.at[c, x, q0 + zh, :, pl.ds(Z0, ZW)], ls.at[15]),
    )
    for cp in own:
        cp.start()
    pl.semaphore_wait(bar, len(peers))
    for cp in own:
        cp.wait()

    def ysl(yy):
        return pl.ds(pl.multiple_of(Y0 + YW * yy, 128), YW)

    def zq(zz):
        return 2 * lax.rem(zz, 2) + zz // 2

    def same(ref, to):
        return send(ref, ref, to)

    xs, zs = pl.ds(0, XW), pl.ds(Z0, ZW)
    za, zb = pl.ds(Z0, ZW // 2), pl.ds(Z0 + ZW // 2, ZW // 2)

    def greet(sem, to):
        for dev in to:
            pl.semaphore_signal(sem, inc=1, device_id=dev, device_id_type=MESH)

    def fold(v, op):
        r = v[:, 0:128]
        for n in range(1, 20):
            r = op(r, v[:, 128 * n : 128 * n + 128])
        return r

    def tea_cols(j):
        return tv[j].astype(F32)

    def tea_max():
        top = lax.fori_loop(
            0, 32, lambda j, m: jnp.maximum(m, fold(tea_cols(j), jnp.maximum)), jnp.full((6, 128), -jnp.inf, F32))
        return jnp.max(top, axis=1, keepdims=True)

    def tea_sum(m):
        tot = lax.fori_loop(
            0, 32, lambda j, s: s + fold(jnp.exp(tea_cols(j) - m), jnp.add), jnp.zeros((6, 128), F32))
        return jnp.sum(tot, axis=1, keepdims=True)

    def tea_write(m, s, lo, hi):
        inv = 1.0 / s
        pad = jnp.zeros((2, 128), F32)

        def block(j, carry):
            p = jnp.exp(tea_cols(bmap[j]) - m) * inv
            for n in range(4):
                rows = [p[:, 640 * n + 128 * i : 640 * n + 128 * i + 128] for i in range(5)]
                mt[2 * j + n // 2, n % 2] = jnp.concatenate(rows + [pad], axis=0).astype(BF16)
            return carry

        lax.fori_loop(lo, hi, block, 0)

    chip = lax.div(me, 2)

    def give(lo, hi):
        def one(i, carry):
            t = lax.rem(chip + i, 64)
            pltpu.make_async_remote_copy(
                src_ref=mt.at[t], dst_ref=rr.at[chip], send_sem=tss, recv_sem=trs,
                device_id=(lax.div(t, 8), 2 * lax.rem(t, 8) + c), device_id_type=MESH,
            ).start()
            return carry

        lax.fori_loop(lo, hi, one, 0)

    class Ring:
        def __init__(self, near, at, part, half, own_to_sib=True):
            self.near, self.at, self.part, self.half, self.own_to_sib = near, at, part, half, own_to_sib

        def start(self):
            ref = self.part(self.at)
            self.right, self.left = same(ref, self.near(1)), same(ref, self.near(3))
            self.own = same(ref, sib) if self.own_to_sib else None

        def forward(self):
            before, after = rot(self.at, 3), rot(self.at, 1)
            arrive(self.right)
            self.far = [same(self.half(before, 0), self.near(1))]
            arrive(self.left)
            self.far.append(same(self.half(after, 1), self.near(3)))
            self.sides = [same(self.part(before), sib), same(self.part(after), sib)]

        def finish(self):
            arrive(*self.far)
            self.end = same(self.part(rot(self.at, 2)), sib)

    def xring(q, own_to_sib):
        return Ring(
            xn, x, lambda v: hb.at[c, v, pl.ds(q, 2), :, xs], lambda v, i: hb.at[c, v, q + i, :, xs], own_to_sib)

    def yring(q):
        return Ring(
            yn, y, lambda v: hb.at[c, :, pl.ds(q, 2), :, ysl(v)],
            lambda v, i: hb.at[c, pl.ds(2 * i, 2), pl.ds(q, 2), :, ysl(v)])

    def zring(cols):
        return Ring(
            zn, z, lambda v: hb.at[c, :, zq(v), :, cols], lambda v, i: hb.at[c, pl.ds(2 * i, 2), zq(v), :, cols])

    xra, xrb = xring(q0, False), xring(qo, True)
    yra, yrb = yring(q0), yring(qo)
    zra, zrb = zring(za), zring(zb)

    def mul_x(h, xx):
        lhs = hb[h, xx, :, :, xs].reshape(192, XW)
        rows = pl.ds(pl.multiple_of(192 * xx, 64), 192)
        acc[rows, :] += jnp.dot(lhs, wb[h, xs, :], preferred_element_type=F32)

    def mul_y(h, yy):
        lhs = hb[h, :, :, :, ysl(yy)].reshape(768, YW)
        acc[...] += jnp.dot(lhs, wb[h, ysl(yy), :], preferred_element_type=F32)

    def mul_z(h, zz):
        q = zq(zz)
        lhs = hb[h, :, q, :, zs].reshape(192, ZW)
        res = jnp.dot(lhs, wb[h, zs, :], preferred_element_type=F32)
        for xx in range(4):
            rows = pl.ds(pl.multiple_of(192 * xx + 48 * q, 16), 48)
            acc[rows, :] += res[48 * xx : 48 * xx + 48]

    def make_perm(p):
        for a in range(6):
            i = lax.broadcasted_iota(jnp.int32, (128, 1), 0) + 128 * a
            n = (i * 43691) >> 19
            k = i - 12 * n
            core = jnp.where(k >= 6, 1, 0)
            first, second, third = n >> 4, (n >> 2) & 3, n & 3
            rx, ry, rz = ((first, second, third), (second, third, first))[p]
            row = 6 * ((rx * 2 + (rz & 1)) * 16 + (rz >> 1) * 8 + ry * 2 + core) + k - 6 * core
            lane = lax.broadcasted_iota(jnp.int32, (128, 128), 1)
            token = jnp.zeros((128, 128), F32)
            for b in range(6):
                token += jnp.where(lane == row - 128 * b, tok[b : b + 1, :].astype(F32), 0.0)
            token = jnp.sum(token, axis=1, keepdims=True)
            col = lax.broadcasted_iota(jnp.int32, (128, 768), 1)
            perm[p, 128 * a : 128 * a + 128, :] = jnp.where(col.astype(F32) == token, 1.0, 0.0).astype(BF16)

    own2, two = pl.ds(q0, 2), pl.ds(qo, 2)
    y1 = [same(hb.at[c, x, own2, :, ysl(y)], xn(d)) for d in (1, 3, 2)]
    py = (same(hb.at[c, x, q0, :, ysl(y)], zn(1)), same(hb.at[c, x, q0 + 1, :, ysl(y)], zn(3)))
    za1 = [same(hb.at[c, x, zq(z), :, za], xn(d)) for d in (1, 3, 2)]
    zb1 = [same(hb.at[c, x, zq(z), :, zb], xn(d)) for d in (1, 3, 2)]
    px = (same(hb.at[c, x, q0, :, xs], zn(1)), same(hb.at[c, x, q0 + 1, :, xs], zn(3)))
    greet(hx, [xn(d) for d in (1, 3, 2)])
    def fetch(j, carry):
        cols = pl.ds(pl.multiple_of(j * HALF, 128), HALF)
        pltpu.make_async_copy(tea.at[:, cols], tv.at[j], ls.at[3]).start()
        return carry

    lax.fori_loop(0, 32, fetch, 0)
    tcopy = pltpu.make_async_copy(tv, tv, ls.at[3])
    other = pltpu.make_async_copy(
        hid.at[:, :, pl.ds(pl.multiple_of(HALF * o, 128), XW)],
        hb.at[o, x, pl.ds(q0, 2), :, pl.ds(0, XW)], ls.at[1])
    other.start()
    wcopy = pltpu.make_async_copy(w, wb, ls.at[2])
    wcopy.start()
    w2copy = pltpu.make_async_copy(w.at[c], wc.at[:, pl.ds(0, 640)], ls.at[16])
    w2copy.start()
    wx = send(w.at[o], wc.at[:, pl.ds(640, 640)], sib)
    tcopy.wait()
    tm = tea_max()
    arrive(*py)
    y2 = [same(hb.at[c, x, two, :, ysl(y)], xn(d)) for d in (1, 3, 2)]
    pl.semaphore_wait(hx, 3)
    greet(hy, [yn(d) for d in (1, 3, 2)])
    arrive(*y1)
    yra.start()
    arrive(*za1)
    zra.start()
    xra.start()
    ts = tea_sum(tm)
    pl.semaphore_wait(hy, 3)
    arrive(*px)
    xrb.start()
    tea_write(tm, ts, 0, 16)
    arrive(*y2)
    yrb.start()
    arrive(*zb1)
    zrb.start()
    tea_write(tm, ts, 16, 32)
    rr[chip] = mt[chip]
    yra.forward()
    zra.forward()
    xra.forward()
    wcopy.wait()
    acc[...] = jnp.zeros_like(acc)
    mul_x(c, x)
    mul_z(c, z)
    xrb.forward()
    yrb.forward()
    zrb.forward()
    mul_y(c, y)
    other.wait()
    arrive(xrb.own)
    mul_x(o, x)
    arrive(zra.own, zrb.own)
    mul_z(o, z)
    arrive(yra.own, yrb.own)
    mul_y(o, y)
    for d in (3, 1):
        mul_x(c, rot(x, d))
        mul_y(c, rot(y, d))
        mul_z(c, rot(z, d))
    xra.finish()
    xrb.finish()
    mul_x(c, rot(x, 2))
    yra.finish()
    zra.finish()
    for i, d in enumerate((3, 1)):
        arrive(xra.sides[i], xrb.sides[i])
        mul_x(o, rot(x, d))
        arrive(yra.sides[i], yrb.sides[i])
        mul_y(o, rot(y, d))
        arrive(zra.sides[i], zrb.sides[i])
        mul_z(o, rot(z, d))
    yrb.finish()
    zrb.finish()
    give(1, 64)
    mul_y(c, rot(y, 2))
    mul_z(c, rot(z, 2))
    arrive(xra.end, xrb.end)
    mul_x(o, rot(x, 2))
    arrive(yra.end, yrb.end)
    mul_y(o, rot(y, 2))
    arrive(zra.end, zrb.end)
    mul_z(o, rot(z, 2))

    eye = lax.broadcasted_iota(jnp.int32, (128, 128), 0) == lax.broadcasted_iota(jnp.int32, (128, 128), 1)
    st0[...] = jnp.zeros_like(st0)

    def to_row(v):
        return jnp.sum(jnp.where(eye, v, 0.0), axis=0, keepdims=True)

    def to_col(v):
        return jnp.sum(jnp.where(eye, v, 0.0), axis=1, keepdims=True)

    for a in range(6):
        rows = slice(128 * a, 128 * a + 128)
        l = acc[rows, :]
        m = jnp.max(l, axis=1, keepdims=True)
        e = jnp.exp(l - m)
        acc[rows, :] = e
        st0[a : a + 1, :] = to_row(m)
        st0[8 + a : 9 + a, :] = to_row(jnp.sum(e, axis=1, keepdims=True))

    def merge(first, ref, n):
        m = first[0:8]
        for k in range(1, n):
            m = jnp.maximum(m, ref[k, 0:8, :])
        s = first[8:16] * jnp.exp(first[0:8] - m)
        for k in range(1, n):
            s += ref[k, 8:16, :] * jnp.exp(ref[k, 0:8, :] - m)
        return m, s

    cps = []
    for d in range(4):
        for e in range(2):
            if d + e > 0:
                to = device(rot(x, d), y, z, c if e == 0 else o)
                cps.append(send(st0, st1.at[2 * d + e], to))
    make_perm(0)
    arrive(*cps)
    m, s = merge(st0[...], st1, 8)
    st2[0, 0:8, :] = m
    st2[0, 8:16, :] = s
    cps = []
    for d in range(4):
        for e in range(4):
            if d + e > 0:
                cps.append(send(st2.at[0], st2.at[4 * d + e], device(x, rot(y, d), rot(z, e), c)))

    whole = pltpu.make_async_remote_copy(
        src_ref=mt.at[pl.ds(0, 63)], dst_ref=rr.at[pl.ds(0, 63)], send_sem=tss, recv_sem=trs,
        device_id=sib, device_id_type=MESH,
    )
    whole.wait_recv()
    cross = send(rr.at[:, o], rt, sib)
    make_perm(1)
    arrive(cross)
    i = lax.broadcasted_iota(jnp.int32, (240, 1), 0)
    j = (i * 1366) >> 16
    k = i - 48 * j
    t = (k * 43) >> 8
    want = t * 32 + j * 6 + (k - 6 * t)
    pick = jnp.where(lax.broadcasted_iota(jnp.int32, (240, 256), 1) == want, 1.0, 0.0).astype(BF16)

    def place(n, carry):
        a, b = rr[pl.ds(4 * n, 4), c], rt[pl.ds(4 * n, 4)]
        lo, hi = jnp.where(c == 0, a, b), jnp.where(c == 0, b, a)
        src = jnp.concatenate([v[r] for r in range(4) for v in (lo, hi)], axis=0)
        res = jnp.dot(pick, src, preferred_element_type=F32).astype(BF16)
        for jj in range(5):
            qb[pl.ds(pl.multiple_of(48 * n, 16), 48), 128 * jj : 128 * jj + 128] = res[48 * jj : 48 * jj + 48]
        return carry

    lax.fori_loop(0, 16, place, 0)

    arrive(*cps)
    m, s = merge(st2[0], st2, 16)
    scale = ups[...] * jnp.exp(st0[0:6, :] - m[0:6]) / s[0:6]
    for a in range(6):
        rows = slice(128 * a, 128 * a + 128)
        sc = to_col(scale[a : a + 1, :])
        uc = to_col(ups[a : a + 1, :])
        g[rows, :] = (acc[rows, :] * sc - uc * qb[rows, :].astype(F32)).astype(BF16)

    gsend = []
    for p in range(2):
        for a in range(3):
            rows = slice(256 * a, 256 * a + 256)
            gc[p, rows, 0:640] = jnp.dot(perm[p, rows, :], g[...], preferred_element_type=F32).astype(BF16)
        gsend.append(send(gc.at[p, :, pl.ds(0, 640)], gc.at[p, :, pl.ds(640, 640)], sib))
    arrive(wx)
    w2copy.wait()

    co = (x, y, z)
    near = (xn, yn, zn)
    nt = (((1,), (1,)), ((), ()))
    sa, sb, sc3 = {}, {}, {}

    def head_part(n):
        h, k = n // 5, n % 5
        lhs = hb[h, :, :, :, 512 * k : 512 * k + 512].reshape(768, 512)
        res = lax.dot_general(lhs, g[...], (((0,), (0,)), ((), ())), preferred_element_type=F32)
        ghb[512 * n : 512 * n + 512, :] = res.astype(BF16)
        cp = pltpu.make_async_copy(ghb.at[pl.ds(512 * n, 512)], gh.at[pl.ds(512 * n, 512)], ls.at[4 + n])
        cp.start()
        return cp

    def partial(p, start, wd):
        return lax.dot_general(gc[p], wc[start : start + wd, :], nt, preferred_element_type=F32).astype(BF16)

    def stage_a(p, k, res):
        tp, ra, ax = tps[p][k], ras[p][k], AXES[p][0]
        for a in range(4):
            for b in range(4):
                at = 192 * b + 48 * a if p == 1 else 192 * a + 48 * b
                tp[a, b] = res[at : at + 48]
        v, f = co[ax], near[ax]
        on, back = ((1, 3), (3, 1))[k]
        sa[p, k] = [send(tp.at[rot(v, 2)], ra.at[2], f(on)), send(tp.at[rot(v, back)], ra.at[0], f(back))]

    def pass_a(p, k):
        tp, ra, on = tps[p][k], ras[p][k], (1, 3)[k]
        arrive(sa[p, k][0])
        ax = AXES[p][0]
        a = rot(co[ax], on)
        tp[a] = (tp[a].astype(F32) + ra[2].astype(F32)).astype(BF16)
        sa[p, k].append(send(tp.at[a], ra.at[1], near[ax](on)))

    def stage_b(p, k):
        ax = AXES[p][1]
        arrive(*sa[p, k][1:])
        ra = ras[p][k]
        res = tps[p][k][co[AXES[p][0]]].astype(F32) + ra[0].astype(F32) + ra[1].astype(F32)
        tbs[p][k][...] = res.astype(BF16)
        sb[p, k] = [send(tbs[p][k].at[rot(co[ax], d)], rbs[p][k].at[d - 1], near[ax](d)) for d in (1, 3, 2)]

    def window(i):
        return pl.ds(pl.multiple_of(8 * (i + i // 2), 8), 16)

    def stage_c(p, k):
        ax, ay = AXES[p][1:]
        arrive(*sb[p, k])
        rb = rbs[p][k]
        tcs[p][k][...] = tbs[p][k][co[ax]].astype(F32) + rb[0].astype(F32) + rb[1].astype(F32) + rb[2].astype(F32)
        sc3[p, k] = [
            send(tcs[p][k].at[window(rot(co[ay], d))], rcs[p][k].at[d - 1], near[ay](d)) for d in (1, 3, 2)]

    def stage_d(p, k):
        start, wd = UNITS[p][k]
        arrive(*sc3[p, k])
        rc = rcs[p][k]
        fin[:, start : start + wd] = tcs[p][k][window(co[AXES[p][2]]), :] + rc[0] + rc[1] + rc[2]

    heads = []
    for k in range(2):
        for p in range(3):
            if k == 0 and p != 1:
                arrive(gsend[p // 2])
            stage_a(p, k, partial(p // 2, *UNITS[p][k]))
    for p in range(3):
        pass_a(p, 0)
    for n in range(2):
        heads.append(head_part(n))
    for p in range(3):
        pass_a(p, 1)
    for n in range(2, 5):
        heads.append(head_part(n))
    for p in range(3):
        stage_b(p, 0)
    for n in range(5, 8):
        heads.append(head_part(n))
    for p in range(3):
        stage_b(p, 1)
    for p in range(3):
        stage_c(p, 0)
    for n in range(8, 10):
        heads.append(head_part(n))
    for p in range(3):
        stage_d(p, 0)
    for p in range(3):
        stage_c(p, 1)
    for p in range(3):
        stage_d(p, 1)
    arrive(send(fin, fs, sib))
    for p in range(3):
        start, wd = min(u[0] for u in UNITS[p]), sum(u[1] for u in UNITS[p])
        odd = lax.rem(co[AXES[p][2]], 2)
        cols = slice(start, start + wd)
        mine, theirs = fin[:, cols], fs[:, cols]

        def rows_of(v):
            even_rows = jnp.where(c == 0, v[0:6], v[6:12])
            odd_rows = jnp.where(c == 0, v[4:10], v[10:16])
            return jnp.where(odd == 0, even_rows, odd_rows).astype(BF16)

        lo = jnp.where(c == 0, mine, theirs)
        hi = jnp.where(c == 0, theirs, mine)
        gx[:, start : start + wd] = rows_of(lo)
        gx[:, HALF + start : HALF + start + wd] = rows_of(hi)

    for cp in heads:
        cp.wait()
    for cp in sent:
        cp.wait_send()
    whole.wait_send()


def shards(hidden_rows, head_weight, teacher_logits, upstream, block_map, token_order):
    vmem = pl.BlockSpec(memory_space=pltpu.VMEM)
    anyw = pl.BlockSpec(memory_space=pl.ANY)
    def per_unit(shape, dtype):
        return [pltpu.VMEM(shape(wd), dtype) for lane in UNITS for _, wd in lane]

    scratch = [
        pltpu.VMEM((2, 4, 4, 48, HALF), BF16),
        pltpu.VMEM((2, HALF, 640), BF16),
        pltpu.VMEM((HALF, 1280), BF16),
        pltpu.VMEM((768, 640), F32),
        pltpu.VMEM((768, 640), BF16),
        pltpu.VMEM((64, 2, 32, 128), BF16),
        pltpu.VMEM((64, 32, 128), BF16),
        pltpu.VMEM((32, 6, HALF), BF16),
        pltpu.VMEM((64, 2, 32, 128), BF16),
        pltpu.VMEM((768, 640), BF16),
        pltpu.VMEM((16, 128), F32),
        pltpu.VMEM((8, 16, 128), F32),
        pltpu.VMEM((16, 16, 128), F32),
        pltpu.VMEM((2, 768, 768), BF16),
        pltpu.VMEM((2, 768, 1280), BF16),
        pltpu.VMEM((5120, 640), BF16),
        pltpu.VMEM((16, HALF), F32),
        pltpu.VMEM((16, HALF), F32),
        *per_unit(lambda wd: (4, 4, 48, wd), BF16),
        *per_unit(lambda wd: (3, 4, 48, wd), BF16),
        *per_unit(lambda wd: (4, 48, wd), BF16),
        *per_unit(lambda wd: (3, 48, wd), BF16),
        *per_unit(lambda wd: (48, wd), F32),
        *per_unit(lambda wd: (3, 16, wd), F32),
        pltpu.SemaphoreType.DMA((160,)),
        pltpu.SemaphoreType.DMA((160,)),
        pltpu.SemaphoreType.DMA((17,)),
        pltpu.SemaphoreType.DMA,
        pltpu.SemaphoreType.DMA,
        pltpu.SemaphoreType.REGULAR,
        pltpu.SemaphoreType.REGULAR,
    ]
    return pl.pallas_call(
        head_kernel,
        out_shape=(jax.ShapeDtypeStruct((5120, 640), BF16), jax.ShapeDtypeStruct((6, 5120), BF16)),
        in_specs=[anyw, anyw, anyw, pl.BlockSpec(memory_space=pltpu.SMEM), vmem, vmem],
        out_specs=(anyw, vmem),
        scratch_shapes=scratch,
        compiler_params=pltpu.CompilerParams(
            collective_id=0, has_side_effects=True, vmem_limit_bytes=62 << 20),
        name="head_backward",
    )(
        hidden_rows.reshape(2, 48, 5120),
        head_weight.reshape(2, HALF, 640),
        teacher_logits,
        block_map,
        upstream.reshape(6, 128),
        token_order.reshape(6, 128),
    )


def solution(mesh):
    in_specs = (P("dp", None), P(None, ("dp", "vocab")), P(("dp", "vocab"), None), P(), P(), P())
    out_specs = (P(None, ("dp", "vocab")), P(("dp", "vocab"), None))
    return jax.shard_map(shards, mesh=mesh, in_specs=in_specs, out_specs=out_specs, check_vma=False)
```

```python
import jax
import jax.numpy as jnp
from jax import lax
from jax.experimental import pallas as pl
from jax.experimental.pallas import tpu as pltpu
from jax.sharding import PartitionSpec as P

MESH = pl.DeviceIdType.MESH
F32 = jnp.float32
BF16 = jnp.bfloat16
HALF = 2560
XW, YW, ZW = 512, 256, 1024
Y0, Z0 = 512, 1536
UNITS = (((0, 512), (512, 256)), ((768, 512), (1280, 256)), ((1536, 512), (2048, 512)))
AXES = ((0, 1, 2), (1, 0, 2), (2, 0, 1))
PLAN = (
    "T20 O T00 T10",
    "T21 T01 T11 P20",
    "P00 P10 H H",
    "P21 P01 P11 H",
    "H H B20 B00",
    "B10 H H H",
    "B21 B01 B11 C20",
    "C00 C10 H H",
    "D20 D00 D10 C21",
    "C01 C11 D21 D01",
    "D11",
)


def device(x, y, z, c):
    return (x * 2 + lax.rem(z, 2), (z // 2) * 8 + y * 2 + c)


def head_kernel(
    hid, w, tea, bmap, ups, tok, gh, gx,
    hb, wb, wc, acc, qb, rr, rt, tv, mt, g, st0, st1, st2, perm, gc, ghb, fin, fs,
    *rest,
):
    ss, rs, ls, tss, trs, hx, hy = rest[36:]

    def by_unit(n):
        refs = iter(rest[6 * n : 6 * n + 6])
        return [[next(refs) for _ in lane] for lane in UNITS]

    tps, ras, tbs, rbs, tcs, rcs = (by_unit(n) for n in range(6))
    dp = lax.axis_index("dp")
    vo = lax.axis_index("vocab")
    x, zl = dp // 2, lax.rem(dp, 2)
    zh, y, c = vo // 8, lax.rem(vo // 2, 4), lax.rem(vo, 2)
    z = zh * 2 + zl
    o = 1 - c
    me = dp * 16 + vo

    def rot(v, d):
        return lax.rem(v + d, 4)

    def xn(d):
        return device(rot(x, d), y, z, c)

    def yn(d):
        return device(x, rot(y, d), z, c)

    def zn(d):
        return device(x, y, rot(z, d), c)

    sib = device(x, y, z, o)
    sent = []

    def region(body):
        pl.when(me >= 0)(body)

    def send(src, dst, to):
        k = len(sent)
        cp = pltpu.make_async_remote_copy(
            src_ref=src, dst_ref=dst, send_sem=ss.at[k], recv_sem=rs.at[k],
            device_id=to, device_id_type=MESH,
        )
        cp.start()
        sent.append(cp)
        return cp

    def arrive(*cps):
        for cp in cps:
            cp.wait_recv()

    bar = pltpu.get_barrier_semaphore()

    peers = [f(d) for f in (xn, yn, zn) for d in (1, 3, 2)] + [sib]
    for to in peers:
        pl.semaphore_signal(bar, inc=1, device_id=to, device_id_type=MESH)
    q0, qo = 2 * zl, 2 * (1 - zl)
    mine = pl.multiple_of(HALF * c, 128)
    own = (
        pltpu.make_async_copy(hid.at[:, :, pl.ds(mine, XW)], hb.at[c, x, pl.ds(q0, 2), :, pl.ds(0, XW)], ls.at[0]),
        pltpu.make_async_copy(
            hid.at[:, :, pl.ds(pl.multiple_of(mine + Y0 + YW * y, 128), YW)],
            hb.at[c, x, pl.ds(q0, 2), :, pl.ds(pl.multiple_of(Y0 + YW * y, 128), YW)], ls.at[14]),
        pltpu.make_async_copy(
            hid.at[zh, :, pl.ds(pl.multiple_of(mine + Z0, 128), ZW)],
            hb.at[c, x, q0 + zh, :, pl.ds(Z0, ZW)], ls.at[15]),
    )
    for cp in own:
        cp.start()
    pl.semaphore_wait(bar, len(peers))
    for cp in own:
        cp.wait()

    def ysl(yy):
        return pl.ds(pl.multiple_of(Y0 + YW * yy, 128), YW)

    def zq(zz):
        return 2 * lax.rem(zz, 2) + zz // 2

    def same(ref, to):
        return send(ref, ref, to)

    xs, zs = pl.ds(0, XW), pl.ds(Z0, ZW)
    za, zb = pl.ds(Z0, ZW // 2), pl.ds(Z0 + ZW // 2, ZW // 2)

    def greet(sem, to):
        for dev in to:
            pl.semaphore_signal(sem, inc=1, device_id=dev, device_id_type=MESH)

    def fold(v, op):
        r = v[:, 0:128]
        for n in range(1, 20):
            r = op(r, v[:, 128 * n : 128 * n + 128])
        return r

    def tea_cols(j):
        return tv[j].astype(F32)

    def tea_max():
        top = lax.fori_loop(
            0, 32, lambda j, m: jnp.maximum(m, fold(tea_cols(j), jnp.maximum)), jnp.full((6, 128), -jnp.inf, F32))
        return jnp.max(top, axis=1, keepdims=True)

    def tea_sum(m):
        tot = lax.fori_loop(
            0, 32, lambda j, s: s + fold(jnp.exp(tea_cols(j) - m), jnp.add), jnp.zeros((6, 128), F32))
        return jnp.sum(tot, axis=1, keepdims=True)

    def tea_write(m, s, lo, hi):
        inv = 1.0 / s
        pad = jnp.zeros((2, 128), F32)

        def block(j, carry):
            p = jnp.exp(tea_cols(bmap[j]) - m) * inv
            for n in range(4):
                rows = [p[:, 640 * n + 128 * i : 640 * n + 128 * i + 128] for i in range(5)]
                mt[2 * j + n // 2, n % 2] = jnp.concatenate(rows + [pad], axis=0).astype(BF16)
            return carry

        lax.fori_loop(lo, hi, block, 0)

    chip = lax.div(me, 2)

    def give(lo, hi):
        def one(i, carry):
            t = lax.rem(chip + i, 64)
            pltpu.make_async_remote_copy(
                src_ref=mt.at[t], dst_ref=rr.at[chip], send_sem=tss, recv_sem=trs,
                device_id=(lax.div(t, 8), 2 * lax.rem(t, 8) + c), device_id_type=MESH,
            ).start()
            return carry

        lax.fori_loop(lo, hi, one, 0)

    class Ring:
        def __init__(self, near, at, part, half, own_to_sib=True):
            self.near, self.at, self.part, self.half, self.own_to_sib = near, at, part, half, own_to_sib

        def start(self):
            ref = self.part(self.at)
            self.right, self.left = same(ref, self.near(1)), same(ref, self.near(3))
            self.own = same(ref, sib) if self.own_to_sib else None

        def forward(self):
            before, after = rot(self.at, 3), rot(self.at, 1)
            arrive(self.right)
            self.far = [same(self.half(before, 0), self.near(1))]
            arrive(self.left)
            self.far.append(same(self.half(after, 1), self.near(3)))
            self.sides = [same(self.part(before), sib), same(self.part(after), sib)]

        def finish(self):
            arrive(*self.far)
            self.end = same(self.part(rot(self.at, 2)), sib)

    def xring(q, own_to_sib):
        return Ring(
            xn, x, lambda v: hb.at[c, v, pl.ds(q, 2), :, xs], lambda v, i: hb.at[c, v, q + i, :, xs], own_to_sib)

    def yring(q):
        return Ring(
            yn, y, lambda v: hb.at[c, :, pl.ds(q, 2), :, ysl(v)],
            lambda v, i: hb.at[c, pl.ds(2 * i, 2), pl.ds(q, 2), :, ysl(v)])

    def zring(cols):
        return Ring(
            zn, z, lambda v: hb.at[c, :, zq(v), :, cols], lambda v, i: hb.at[c, pl.ds(2 * i, 2), zq(v), :, cols])

    xra, xrb = xring(q0, False), xring(qo, True)
    yra, yrb = yring(q0), yring(qo)
    zra, zrb = zring(za), zring(zb)

    def mul_x(h, xx):
        @region
        def _():
            lhs = hb[h, xx, :, :, xs].reshape(192, XW)
            rows = pl.ds(pl.multiple_of(192 * xx, 64), 192)
            acc[rows, :] += jnp.dot(lhs, wb[h, xs, :], preferred_element_type=F32)

    def mul_y(h, yy):
        @region
        def _():
            lhs = hb[h, :, :, :, ysl(yy)].reshape(768, YW)
            acc[...] += jnp.dot(lhs, wb[h, ysl(yy), :], preferred_element_type=F32)

    def mul_z(h, zz):
        @region
        def _():
            q = zq(zz)
            lhs = hb[h, :, q, :, zs].reshape(192, ZW)
            res = jnp.dot(lhs, wb[h, zs, :], preferred_element_type=F32)
            for xx in range(4):
                rows = pl.ds(pl.multiple_of(192 * xx + 48 * q, 16), 48)
                acc[rows, :] += res[48 * xx : 48 * xx + 48]

    def make_perm(p):
        for a in range(6):
            i = lax.broadcasted_iota(jnp.int32, (128, 1), 0) + 128 * a
            n = (i * 43691) >> 19
            k = i - 12 * n
            core = jnp.where(k >= 6, 1, 0)
            first, second, third = n >> 4, (n >> 2) & 3, n & 3
            rx, ry, rz = ((first, second, third), (second, third, first))[p]
            row = 6 * ((rx * 2 + (rz & 1)) * 16 + (rz >> 1) * 8 + ry * 2 + core) + k - 6 * core
            lane = lax.broadcasted_iota(jnp.int32, (128, 128), 1)
            token = jnp.zeros((128, 128), F32)
            for b in range(6):
                token += jnp.where(lane == row - 128 * b, tok[b : b + 1, :].astype(F32), 0.0)
            token = jnp.sum(token, axis=1, keepdims=True)
            col = lax.broadcasted_iota(jnp.int32, (128, 768), 1)
            perm[p, 128 * a : 128 * a + 128, :] = jnp.where(col.astype(F32) == token, 1.0, 0.0).astype(BF16)

    own2, two = pl.ds(q0, 2), pl.ds(qo, 2)
    y1 = [same(hb.at[c, x, own2, :, ysl(y)], xn(d)) for d in (1, 3, 2)]
    py = (same(hb.at[c, x, q0, :, ysl(y)], zn(1)), same(hb.at[c, x, q0 + 1, :, ysl(y)], zn(3)))
    za1 = [same(hb.at[c, x, zq(z), :, za], xn(d)) for d in (1, 3, 2)]
    zb1 = [same(hb.at[c, x, zq(z), :, zb], xn(d)) for d in (1, 3, 2)]
    px = (same(hb.at[c, x, q0, :, xs], zn(1)), same(hb.at[c, x, q0 + 1, :, xs], zn(3)))
    greet(hx, [xn(d) for d in (1, 3, 2)])
    def fetch(j, carry):
        cols = pl.ds(pl.multiple_of(j * HALF, 128), HALF)
        pltpu.make_async_copy(tea.at[:, cols], tv.at[j], ls.at[3]).start()
        return carry

    lax.fori_loop(0, 32, fetch, 0)
    tcopy = pltpu.make_async_copy(tv, tv, ls.at[3])
    other = pltpu.make_async_copy(
        hid.at[:, :, pl.ds(pl.multiple_of(HALF * o, 128), XW)],
        hb.at[o, x, pl.ds(q0, 2), :, pl.ds(0, XW)], ls.at[1])
    other.start()
    wcopy = pltpu.make_async_copy(w, wb, ls.at[2])
    wcopy.start()
    w2copy = pltpu.make_async_copy(w.at[c], wc.at[:, pl.ds(0, 640)], ls.at[16])
    w2copy.start()
    wx = send(w.at[o], wc.at[:, pl.ds(640, 640)], sib)
    tcopy.wait()
    tm = tea_max()
    arrive(*py)
    y2 = [same(hb.at[c, x, two, :, ysl(y)], xn(d)) for d in (1, 3, 2)]
    pl.semaphore_wait(hx, 3)
    greet(hy, [yn(d) for d in (1, 3, 2)])
    arrive(*y1)
    yra.start()
    arrive(*za1)
    zra.start()
    xra.start()
    ts = tea_sum(tm)
    pl.semaphore_wait(hy, 3)
    arrive(*px)
    xrb.start()
    tea_write(tm, ts, 0, 16)
    arrive(*y2)
    yrb.start()
    arrive(*zb1)
    zrb.start()
    tea_write(tm, ts, 16, 32)
    rr[chip] = mt[chip]
    give(1, 20)
    yra.forward()
    zra.forward()
    xra.forward()
    wcopy.wait()
    acc[...] = jnp.zeros_like(acc)
    mul_x(c, x)
    mul_z(c, z)
    xrb.forward()
    yrb.forward()
    zrb.forward()
    mul_y(c, y)
    region(lambda: make_perm(0))
    region(lambda: make_perm(1))
    other.wait()
    arrive(xrb.own)
    mul_x(o, x)
    arrive(zra.own, zrb.own)
    mul_z(o, z)
    arrive(yra.own, yrb.own)
    mul_y(o, y)
    for d in (3, 1):
        mul_x(c, rot(x, d))
        mul_y(c, rot(y, d))
        mul_z(c, rot(z, d))
    xra.finish()
    xrb.finish()
    mul_x(c, rot(x, 2))
    yra.finish()
    zra.finish()
    for i, d in enumerate((3, 1)):
        arrive(xra.sides[i], xrb.sides[i])
        mul_x(o, rot(x, d))
        arrive(yra.sides[i], yrb.sides[i])
        mul_y(o, rot(y, d))
        arrive(zra.sides[i], zrb.sides[i])
        mul_z(o, rot(z, d))
    yrb.finish()
    zrb.finish()
    give(20, 64)
    mul_y(c, rot(y, 2))
    mul_z(c, rot(z, 2))
    arrive(xra.end, xrb.end)
    mul_x(o, rot(x, 2))
    arrive(yra.end, yrb.end)
    mul_y(o, rot(y, 2))
    arrive(zra.end, zrb.end)
    mul_z(o, rot(z, 2))

    eye = lax.broadcasted_iota(jnp.int32, (128, 128), 0) == lax.broadcasted_iota(jnp.int32, (128, 128), 1)
    st0[...] = jnp.zeros_like(st0)

    def to_row(v):
        return jnp.sum(jnp.where(eye, v, 0.0), axis=0, keepdims=True)

    def to_col(v):
        return jnp.sum(jnp.where(eye, v, 0.0), axis=1, keepdims=True)

    for a in range(6):
        rows = slice(128 * a, 128 * a + 128)
        l = acc[rows, :]
        m = jnp.max(l, axis=1, keepdims=True)
        e = jnp.exp(l - m)
        acc[rows, :] = e
        st0[a : a + 1, :] = to_row(m)
        st0[8 + a : 9 + a, :] = to_row(jnp.sum(e, axis=1, keepdims=True))

    def merge(first, ref, n):
        m = first[0:8]
        for k in range(1, n):
            m = jnp.maximum(m, ref[k, 0:8, :])
        s = first[8:16] * jnp.exp(first[0:8] - m)
        for k in range(1, n):
            s += ref[k, 8:16, :] * jnp.exp(ref[k, 0:8, :] - m)
        return m, s

    cps = []
    for d in range(4):
        for e in range(2):
            if d + e > 0:
                to = device(rot(x, d), y, z, c if e == 0 else o)
                cps.append(send(st0, st1.at[2 * d + e], to))
    arrive(*cps)
    m, s = merge(st0[...], st1, 8)
    st2[0, 0:8, :] = m
    st2[0, 8:16, :] = s
    cps = []
    for d in range(4):
        for e in range(4):
            if d + e > 0:
                cps.append(send(st2.at[0], st2.at[4 * d + e], device(x, rot(y, d), rot(z, e), c)))

    whole = pltpu.make_async_remote_copy(
        src_ref=mt.at[pl.ds(0, 63)], dst_ref=rr.at[pl.ds(0, 63)], send_sem=tss, recv_sem=trs,
        device_id=sib, device_id_type=MESH,
    )
    whole.wait_recv()
    cross = send(rr.at[:, o], rt, sib)
    arrive(cross)
    i = lax.broadcasted_iota(jnp.int32, (240, 1), 0)
    j = (i * 1366) >> 16
    k = i - 48 * j
    t = (k * 43) >> 8
    want = t * 32 + j * 6 + (k - 6 * t)
    pick = jnp.where(lax.broadcasted_iota(jnp.int32, (240, 256), 1) == want, 1.0, 0.0).astype(BF16)

    def place(n, carry):
        a, b = rr[pl.ds(4 * n, 4), c], rt[pl.ds(4 * n, 4)]
        lo, hi = jnp.where(c == 0, a, b), jnp.where(c == 0, b, a)
        src = jnp.concatenate([v[r] for r in range(4) for v in (lo, hi)], axis=0)
        res = jnp.dot(pick, src, preferred_element_type=F32).astype(BF16)
        for jj in range(5):
            qb[pl.ds(pl.multiple_of(48 * n, 16), 48), 128 * jj : 128 * jj + 128] = res[48 * jj : 48 * jj + 48]
        return carry

    lax.fori_loop(0, 16, place, 0)

    arrive(*cps)
    m, s = merge(st2[0], st2, 16)
    scale = ups[...] * jnp.exp(st0[0:6, :] - m[0:6]) / s[0:6]
    gsend = []
    for a in range(6):
        rows = slice(128 * a, 128 * a + 128)
        sc = to_col(scale[a : a + 1, :])
        uc = to_col(ups[a : a + 1, :])
        g[rows, 0:640] = (acc[rows, :] * sc - uc * qb[rows, :].astype(F32)).astype(BF16)
        if a % 2 == 1:
            part = pl.ds(128 * (a - 1), 256)
            gsend.append(send(g.at[part, pl.ds(0, 640)], g.at[part, pl.ds(640, 640)], sib))

    def order(p):
        @region
        def _():
            for a in range(3):
                rows = slice(256 * a, 256 * a + 256)
                gc[p, rows, :] = jnp.dot(perm[p, rows, :], g[...], preferred_element_type=F32).astype(BF16)

    co = (x, y, z)
    near = (xn, yn, zn)
    nt = (((1,), (1,)), ((), ()))
    sa, sb, sc3 = {}, {}, {}

    def head_part(n):
        h, k = n // 5, n % 5

        @region
        def _():
            lhs = hb[h, :, :, :, 512 * k : 512 * k + 512].reshape(768, 512)
            res = lax.dot_general(lhs, g[:, 0:640], (((0,), (0,)), ((), ())), preferred_element_type=F32)
            ghb[512 * n : 512 * n + 512, :] = res.astype(BF16)

        cp = pltpu.make_async_copy(ghb.at[pl.ds(512 * n, 512)], gh.at[pl.ds(512 * n, 512)], ls.at[4 + n])
        cp.start()
        return cp

    def partial(p, k):
        (start, wd), tp, ra, ax = UNITS[p][k], tps[p][k], ras[p][k], AXES[p][0]

        @region
        def _():
            res = lax.dot_general(gc[p // 2], wc[start : start + wd, :], nt, preferred_element_type=F32)
            res = res.astype(BF16)
            for a in range(4):
                for b in range(4):
                    at = 192 * b + 48 * a if p == 1 else 192 * a + 48 * b
                    tp[a, b] = res[at : at + 48]

        v, f = co[ax], near[ax]
        on, back = ((1, 3), (3, 1))[k % 2]
        sa[p, k] = [send(tp.at[rot(v, 2)], ra.at[2], f(on)), send(tp.at[rot(v, back)], ra.at[0], f(back))]

    def pass_a(p, k):
        tp, ra, on = tps[p][k], ras[p][k], (1, 3)[k % 2]
        arrive(sa[p, k][0])
        ax = AXES[p][0]
        a = rot(co[ax], on)
        tp[a] = (tp[a].astype(F32) + ra[2].astype(F32)).astype(BF16)
        sa[p, k].append(send(tp.at[a], ra.at[1], near[ax](on)))

    def stage_b(p, k):
        ax = AXES[p][1]
        arrive(*sa[p, k][1:])
        ra = ras[p][k]
        res = tps[p][k][co[AXES[p][0]]].astype(F32) + ra[0].astype(F32) + ra[1].astype(F32)
        tbs[p][k][...] = res.astype(BF16)
        sb[p, k] = [send(tbs[p][k].at[rot(co[ax], d)], rbs[p][k].at[d - 1], near[ax](d)) for d in (1, 3, 2)]

    def window(i):
        return pl.ds(pl.multiple_of(8 * (i + i // 2), 8), 16)

    def stage_c(p, k):
        ax, ay = AXES[p][1:]
        arrive(*sb[p, k])
        rb = rbs[p][k]
        tcs[p][k][...] = tbs[p][k][co[ax]].astype(F32) + rb[0].astype(F32) + rb[1].astype(F32) + rb[2].astype(F32)
        sc3[p, k] = [
            send(tcs[p][k].at[window(rot(co[ay], d))], rcs[p][k].at[d - 1], near[ay](d)) for d in (1, 3, 2)]

    def stage_d(p, k):
        start, wd = UNITS[p][k]
        arrive(*sc3[p, k])
        rc = rcs[p][k]
        fin[:, start : start + wd] = tcs[p][k][window(co[AXES[p][2]]), :] + rc[0] + rc[1] + rc[2]

    heads = []
    arrive(*gsend, wx)
    w2copy.wait()
    order(1)
    steps = {"T": partial, "P": pass_a, "B": stage_b, "C": stage_c, "D": stage_d}
    for step in [step for group in PLAN for step in group.split()]:
        if step == "O":
            order(0)
        elif step == "H":
            heads.append(head_part(len(heads)))
        else:
            steps[step[0]](int(step[1]), int(step[2]))
    arrive(send(fin, fs, sib))
    for p in range(3):
        start, wd = UNITS[p][0][0], sum(u[1] for u in UNITS[p])
        odd = lax.rem(co[AXES[p][2]], 2)
        cols = slice(start, start + wd)
        mine, theirs = fin[:, cols], fs[:, cols]

        def rows_of(v):
            even_rows = jnp.where(c == 0, v[0:6], v[6:12])
            odd_rows = jnp.where(c == 0, v[4:10], v[10:16])
            return jnp.where(odd == 0, even_rows, odd_rows).astype(BF16)

        lo = jnp.where(c == 0, mine, theirs)
        hi = jnp.where(c == 0, theirs, mine)
        gx[:, start : start + wd] = rows_of(lo)
        gx[:, HALF + start : HALF + start + wd] = rows_of(hi)

    for cp in heads:
        cp.wait()
    for cp in sent:
        cp.wait_send()
    whole.wait_send()


def shards(hidden_rows, head_weight, teacher_logits, upstream, block_map, token_order):
    vmem = pl.BlockSpec(memory_space=pltpu.VMEM)
    anyw = pl.BlockSpec(memory_space=pl.ANY)
    def per_unit(shape, dtype):
        return [pltpu.VMEM(shape(wd), dtype) for lane in UNITS for _, wd in lane]

    scratch = [
        pltpu.VMEM((2, 4, 4, 48, HALF), BF16),
        pltpu.VMEM((2, HALF, 640), BF16),
        pltpu.VMEM((HALF, 1280), BF16),
        pltpu.VMEM((768, 640), F32),
        pltpu.VMEM((768, 640), BF16),
        pltpu.VMEM((64, 2, 32, 128), BF16),
        pltpu.VMEM((64, 32, 128), BF16),
        pltpu.VMEM((32, 6, HALF), BF16),
        pltpu.VMEM((64, 2, 32, 128), BF16),
        pltpu.VMEM((768, 1280), BF16),
        pltpu.VMEM((16, 128), F32),
        pltpu.VMEM((8, 16, 128), F32),
        pltpu.VMEM((16, 16, 128), F32),
        pltpu.VMEM((2, 768, 768), BF16),
        pltpu.VMEM((2, 768, 1280), BF16),
        pltpu.VMEM((5120, 640), BF16),
        pltpu.VMEM((16, HALF), F32),
        pltpu.VMEM((16, HALF), F32),
        *per_unit(lambda wd: (4, 4, 48, wd), BF16),
        *per_unit(lambda wd: (3, 4, 48, wd), BF16),
        *per_unit(lambda wd: (4, 48, wd), BF16),
        *per_unit(lambda wd: (3, 48, wd), BF16),
        *per_unit(lambda wd: (48, wd), F32),
        *per_unit(lambda wd: (3, 16, wd), F32),
        pltpu.SemaphoreType.DMA((192,)),
        pltpu.SemaphoreType.DMA((192,)),
        pltpu.SemaphoreType.DMA((17,)),
        pltpu.SemaphoreType.DMA,
        pltpu.SemaphoreType.DMA,
        pltpu.SemaphoreType.REGULAR,
        pltpu.SemaphoreType.REGULAR,
    ]
    return pl.pallas_call(
        head_kernel,
        out_shape=(jax.ShapeDtypeStruct((5120, 640), BF16), jax.ShapeDtypeStruct((6, 5120), BF16)),
        in_specs=[anyw, anyw, anyw, pl.BlockSpec(memory_space=pltpu.SMEM), vmem, vmem],
        out_specs=(anyw, vmem),
        scratch_shapes=scratch,
        compiler_params=pltpu.CompilerParams(
            collective_id=0, has_side_effects=True, vmem_limit_bytes=62 << 20),
        name="head_backward",
    )(
        hidden_rows.reshape(2, 48, 5120),
        head_weight.reshape(2, HALF, 640),
        teacher_logits,
        block_map,
        upstream.reshape(6, 128),
        token_order.reshape(6, 128),
    )


def solution(mesh):
    in_specs = (P("dp", None), P(None, ("dp", "vocab")), P(("dp", "vocab"), None), P(), P(), P())
    out_specs = (P(None, ("dp", "vocab")), P(("dp", "vocab"), None))
    return jax.shard_map(shards, mesh=mesh, in_specs=in_specs, out_specs=out_specs, check_vma=False)
```
